32 devices in a mesh: mom: 2 (over y), shard: 16 (over z, x, core).
Axes of the slice: x: 2, y: 2, z: 4, core: 2. Of those that a mesh axis runs over, the one named last changes fastest.
Arguments:
- green_ret: bfloat16 [2, 256, 8, 2, 128, 128], P('mom', 'shard'), may hold values from -4 to 4
- broadening: bfloat16 [2, 128, 128], replicated, may hold values from -0.5 to 0.5
- occupation: float32 [2, 256], P('mom', 'shard'), may hold values from 0.1 to 1
- neighbours: int32 [64, 4], replicated, may hold values from 0 to 63, as said below
- orbitals: int32 [64], replicated, may hold values from 4 to 16
- coupling: bfloat16 [64, 4, 256, 256], P('shard'), may hold values from -0.1875 to 0.1875
- phonon: float32 [8, 2, 256], replicated, may hold values from -5 to 5
- mode_table: int32 [2, 2], replicated, may hold values from 0 to 7, as said below
Outputs:
- self_energy: bfloat16 [2, 256, 64, 2, 256], P('mom', None, 'shard')
The draws below stay inside these ranges and needn't reach their ends.
Inputs may be any that keep to these rules, and one draw needn't show every extreme that they name: `neighbours`: row a holds 4 distinct atoms of a's own layer block (atoms 8 * (a // 8) onward), none equal to a; the first is a with its lowest bit flipped. `mode_table`: each entry names one of the 8 phonon modes.
All inputs are finite; a program needn't handle non-finite values.
Results may differ from the reference program's by a relative error of at most 0.013.
Values may be sent and summed in bfloat16 or wider, within the bound.
A program may use at most 192 MiB of HBM per device.

```python
import math
import jax
import jax.numpy as jnp
import numpy as np
from jax import lax

NORB = 16
ATL = 8
NBR = 4
MODES = 8
ENERGIES = 256
LAYERS = 8
ORB = 128
PAIR = 256
ATOMS = 64
KPTS = 2


def draw_neighbours(key, part):
    candidate_rows = np.array([[column_slot for column_slot in range(ATL) if column_slot != atom_slot and column_slot != atom_slot ^ 1] for atom_slot in range(ATL)], dtype=np.int32)
    atom_ids = jnp.arange(ATOMS, dtype=jnp.int32)
    in_layer = atom_ids % ATL
    layer_start = atom_ids - in_layer
    candidates = jnp.asarray(candidate_rows)[in_layer]
    scores = jax.random.randint(key, (ATOMS, ATL - 2), 0, 1 << 20, dtype=jnp.int32) * (ATL - 2) + jnp.arange(ATL - 2, dtype=jnp.int32)[None, :]
    ordering = jnp.argsort(scores, axis=1)
    chosen = jnp.take_along_axis(candidates, ordering[:, :NBR - 1], axis=1)
    partner = layer_start + jnp.bitwise_xor(in_layer, 1)
    return jnp.concatenate([partner[:, None], layer_start[:, None] + chosen], axis=1).astype(jnp.int32)


def draw_mode_table(key, part):
    table_key = jax.random.fold_in(key, 7)
    drawn = jax.random.randint(table_key, (KPTS, KPTS), 0, MODES, dtype=jnp.int32)
    row_ids = jnp.arange(KPTS, dtype=jnp.int32)[:, None]
    column_ids = jnp.arange(KPTS, dtype=jnp.int32)[None, :]
    pinned = (row_ids == KPTS - 1) & (column_ids == 0)
    return jnp.where(pinned, MODES - 1, drawn).astype(jnp.int32)


def set_ends(values, own_key, smallest, high):
    spot = [jax.random.randint(jax.random.fold_in(own_key, axis), (), 0, length) for axis, length in enumerate(values.shape)]
    longest = values.shape.index(max(values.shape))
    next_to = spot[:longest] + [(spot[longest] + 1) % values.shape[longest]] + spot[longest + 1:]
    return values.at[tuple(spot)].set(smallest).at[tuple(next_to)].set(high)


def block_scale(own_key, extent, cuts, least, high):
    gain = 1.0
    for position, parts in cuts:
        heights = jax.random.uniform(jax.random.fold_in(jax.random.fold_in(own_key, 6), position), (parts,), jnp.float32, least / len(cuts), high / len(cuts))
        gain = gain * jnp.repeat(jnp.exp(heights), extent[position] // parts).reshape((-1,) + (1,) * (len(extent) - 1 - position))
    return gain


def bell_draw(rng, extent, deviation, bound, split=(), kind=jnp.bfloat16):
    gain = block_scale(rng, extent, split, -0.22, 0.18) if split else 1.0
    values = jax.random.normal(rng, extent, jnp.float32) * deviation * gain
    return jnp.minimum(jnp.maximum(values, -bound), bound).astype(kind)


def setup_inputs(seed: int = 0) -> dict:
    seeds = jax.random.split(jax.random.key(seed), 9)
    return {
        "green_ret": bell_draw(seeds[0], (KPTS, ENERGIES, LAYERS, 2, ORB, ORB), 0.3, 4.0, ((0, 2), (1, 16))),
        "broadening": bell_draw(seeds[1], (2, ORB, ORB), ORB ** -0.5, 0.5),
        "occupation": jnp.clip(0.1 + 0.9 * jax.random.uniform(seeds[2], (KPTS, ENERGIES), jnp.float32) ** block_scale(seeds[2], (KPTS, ENERGIES), ((0, 2), (1, 16)), -0.2, 0.2), 0.1, 1.0),
        "neighbours": draw_neighbours(jax.random.fold_in(seeds[8], 71), 0),
        "orbitals": set_ends(jax.random.randint(seeds[4], (ATOMS,), NORB // 4, NORB + 1), jax.random.fold_in(seeds[4], 1), NORB // 4, NORB).astype(jnp.int32),
        "coupling": bell_draw(seeds[5], (ATOMS, NBR, PAIR, PAIR), (NBR * PAIR) ** -0.5, 0.1875, ((0, 16),)),
        "phonon": bell_draw(seeds[6], (MODES, 2, ENERGIES), 0.7, 5.0, (), jnp.float32),
        "mode_table": draw_mode_table(jax.random.fold_in(seeds[8], 71), 0),
    }


def dft_tables(length):
    counter = jnp.arange(length, dtype=jnp.int32)
    phases = (counter[:, None] * counter[None, :]) % length
    angles = phases.astype(jnp.float32) * (2.0 * math.pi / length)
    return jnp.cos(angles).astype(jnp.bfloat16), jnp.sin(angles).astype(jnp.bfloat16)


def settle(values):
    return lax.optimization_barrier(values.astype(jnp.bfloat16)).astype(jnp.float32)


def coupled_block(green_block, occupation_block, broadening, neighbours, orbitals, coupling):
    block_len = green_block.shape[0]
    highest = lax.Precision.HIGHEST
    stacked = jnp.concatenate([broadening[0], broadening[1]], axis=1)
    products = jnp.dot(green_block.reshape(-1, ORB), stacked, preferred_element_type=jnp.float32)
    products = products.reshape(block_len, LAYERS, 2, ORB, 2, ORB)
    left_re = settle(products[:, :, 0, :, 0] - products[:, :, 1, :, 1])
    left_im = settle(products[:, :, 0, :, 1] + products[:, :, 1, :, 0])
    green_full = green_block.astype(jnp.float32)
    green_re = green_full[:, :, 0]
    green_im = green_full[:, :, 1]
    full_re = jnp.einsum('elik,eljk->elij', left_re, green_re, precision=highest) + jnp.einsum('elik,eljk->elij', left_im, green_im, precision=highest)
    full_im = jnp.einsum('elik,eljk->elij', left_im, green_re, precision=highest) - jnp.einsum('elik,eljk->elij', left_re, green_im, precision=highest)
    weight = occupation_block[:, None, None, None]
    stacked_full = jnp.stack([full_re * weight, full_im * weight], axis=2)
    blocks = stacked_full.reshape(block_len, LAYERS, 2, ATL, NORB, ATL, NORB)
    blocks = blocks.transpose(0, 1, 3, 5, 2, 4, 6).reshape(block_len, ATOMS, ATL, 2, NORB, NORB)
    slot_atoms = neighbours % ATL
    chosen = jnp.take_along_axis(blocks, slot_atoms[None, :, :, None, None, None], axis=2)
    counter = jnp.arange(NORB, dtype=jnp.int32)
    row_mask = counter[None, :] < orbitals[:, None]
    column_mask = counter[None, None, :] < orbitals[neighbours][:, :, None]
    pair_mask = (row_mask[:, None, :, None] & column_mask[:, :, None, :]).astype(jnp.float32)
    scaled = chosen * pair_mask[None, :, :, None, :, :]
    pair_blocks = settle(scaled.reshape(block_len, ATOMS, NBR, 2, PAIR))
    mixed_terms = jnp.einsum('eanpx,anxy->eapy', pair_blocks, coupling.astype(jnp.float32), precision=highest)
    pair_index = jnp.arange(PAIR, dtype=jnp.int32)
    own_mask = ((pair_index[None, :] // NORB < orbitals[:, None]) & (pair_index[None, :] % NORB < orbitals[:, None])).astype(jnp.float32)
    return (mixed_terms * own_mask[None, :, None, :]).astype(jnp.bfloat16)


def reference(green_ret, broadening, occupation, neighbours, orbitals, coupling, phonon, mode_table):
    cos_table, sin_table = dft_tables(ENERGIES)
    block_len = math.gcd(ENERGIES, 64)
    block_count = ENERGIES // block_len

    def per_momentum(inputs):
        green_one, occupation_one = inputs

        def one_block(block_in):
            return coupled_block(block_in[0], block_in[1], broadening, neighbours, orbitals, coupling)

        coupled = lax.map(one_block, (green_one.reshape(block_count, block_len, LAYERS, 2, ORB, ORB), occupation_one.reshape(block_count, block_len)))
        flat_coupled = coupled.reshape(ENERGIES, -1)
        part_cos = jnp.dot(cos_table, flat_coupled, preferred_element_type=jnp.float32).reshape(ENERGIES, ATOMS, 2, PAIR)
        part_sin = jnp.dot(sin_table, flat_coupled, preferred_element_type=jnp.float32).reshape(ENERGIES, ATOMS, 2, PAIR)
        timed_re = part_cos[:, :, 0] + part_sin[:, :, 1]
        timed_im = part_cos[:, :, 1] - part_sin[:, :, 0]
        return jnp.stack([timed_re, timed_im], axis=2).astype(jnp.bfloat16)

    time_data = lax.map(per_momentum, (green_ret, occupation))
    time_values = lax.optimization_barrier(time_data).astype(jnp.float32)

    def per_target(target_index):
        kernel = phonon[mode_table[target_index]]
        kernel_re = kernel[:, 0][:, :, None, None]
        kernel_im = kernel[:, 1][:, :, None, None]
        sum_re = jnp.sum(kernel_re * time_values[:, :, :, 0] - kernel_im * time_values[:, :, :, 1], axis=0)
        sum_im = jnp.sum(kernel_re * time_values[:, :, :, 1] + kernel_im * time_values[:, :, :, 0], axis=0)
        convolved = jnp.stack([sum_re, sum_im], axis=2).astype(jnp.bfloat16)
        flat_conv = convolved.reshape(ENERGIES, -1)
        back_cos = jnp.dot(cos_table, flat_conv, preferred_element_type=jnp.float32).reshape(ENERGIES, ATOMS, 2, PAIR)
        back_sin = jnp.dot(sin_table, flat_conv, preferred_element_type=jnp.float32).reshape(ENERGIES, ATOMS, 2, PAIR)
        out_re = (back_cos[:, :, 0] - back_sin[:, :, 1]) * (1.0 / ENERGIES)
        out_im = (back_cos[:, :, 1] + back_sin[:, :, 0]) * (1.0 / ENERGIES)
        return jnp.stack([out_re, out_im], axis=2).astype(jnp.bfloat16)

    return lax.map(per_target, jnp.arange(KPTS, dtype=jnp.int32))
```

```python
import functools
import math

import jax
import jax.numpy as jnp
from jax import lax
from jax.experimental import pallas as pl
from jax.experimental.pallas import tpu as pltpu
from jax.sharding import PartitionSpec as P

NORB = 16
ATL = 8
NBR = 4
ENERGIES = 256
LAYERS = 8
ORB = 128
PAIR = 256
ATOMS = 64


def dft_tables(length):
    counter = jnp.arange(length, dtype=jnp.int32)
    phases = counter[:, None] * counter[None, :] % length
    angles = phases.astype(jnp.float32) * (2.0 * math.pi / length)
    return (jnp.cos(angles).astype(jnp.bfloat16), jnp.sin(angles).astype(jnp.bfloat16))


def local(green_ret, broadening, occupation, neighbours, orbitals, coupling, phonon, mode_table):
    highest = lax.Precision.HIGHEST
    greens = green_ret[0]
    energy_dev = greens.shape[0]
    mixing = jnp.stack(
        [
            jnp.concatenate([broadening[0], broadening[1]], axis=1),
            jnp.concatenate([-broadening[1], broadening[0]], axis=1),
        ],
        axis=0,
    )
    left = jnp.einsum("elpik,pkq->eliq", greens, mixing, preferred_element_type=jnp.float32).astype(
        jnp.bfloat16
    )
    slot_atoms = neighbours % ATL
    selector = slot_atoms[:, :, None] == jnp.arange(ATL, dtype=jnp.int32)[None, None, :]
    layer_orbitals = jnp.repeat(orbitals.reshape(LAYERS, ATL), ATL, axis=0)
    partner_count = jnp.sum(jnp.where(selector, layer_orbitals[:, None, :], 0), axis=2)
    green_rows = greens.reshape(energy_dev, LAYERS, 2, ATL, NORB, ORB)
    select_bf = selector.reshape(LAYERS, ATL, NBR, ATL).astype(jnp.bfloat16)
    partner_rows = jnp.einsum(
        "ljnm,elpmic->eljnpic", select_bf, green_rows, preferred_element_type=jnp.float32
    ).astype(jnp.bfloat16)
    partner_re = partner_rows[:, :, :, :, 0]
    partner_im = partner_rows[:, :, :, :, 1]
    left_rows_re = left[..., :ORB].reshape(energy_dev, LAYERS, ATL, NORB, ORB)
    left_rows_im = left[..., ORB:].reshape(energy_dev, LAYERS, ATL, NORB, ORB)
    pair_re = jnp.einsum(
        "eljic,eljnkc->eljnik", left_rows_re, partner_re, preferred_element_type=jnp.float32
    ) + jnp.einsum(
        "eljic,eljnkc->eljnik", left_rows_im, partner_im, preferred_element_type=jnp.float32
    )
    pair_im = jnp.einsum(
        "eljic,eljnkc->eljnik", left_rows_im, partner_re, preferred_element_type=jnp.float32
    ) - jnp.einsum(
        "eljic,eljnkc->eljnik", left_rows_re, partner_im, preferred_element_type=jnp.float32
    )
    chosen = jnp.stack([pair_re, pair_im], axis=4)
    chosen = chosen.reshape(energy_dev, ATOMS, NBR, 2, NORB, NORB)
    counter = jnp.arange(NORB, dtype=jnp.int32)
    row_mask = counter[None, :] < orbitals[:, None]
    column_mask = counter[None, None, :] < partner_count[:, :, None]
    pair_mask = (row_mask[:, None, :, None] & column_mask[:, :, None, :]).astype(jnp.float32)
    scaled = (
        chosen * occupation[0][:, None, None, None, None, None] * pair_mask[None, :, :, None, :, :]
    )
    pair_blocks = scaled.reshape(energy_dev, ATOMS, NBR, 2, PAIR).astype(jnp.bfloat16)
    arrived = lax.all_to_all(pair_blocks, "shard", split_axis=1, concat_axis=0, tiled=True)
    atom_dev = arrived.shape[1]
    mixed_terms = jnp.einsum(
        "eanpx,anxy->eapy", arrived, coupling, preferred_element_type=jnp.float32
    )
    first_atom = lax.axis_index("shard") * atom_dev
    own_orbitals = lax.dynamic_slice_in_dim(orbitals, first_atom, atom_dev)
    pair_index = jnp.arange(PAIR, dtype=jnp.int32)
    own_mask = (
        (pair_index[None, :] // NORB < own_orbitals[:, None])
        & (pair_index[None, :] % NORB < own_orbitals[:, None])
    ).astype(jnp.float32)
    coupled = (mixed_terms * own_mask[None, :, None, :]).astype(jnp.bfloat16)
    cos_table, sin_table = dft_tables(ENERGIES)
    flat_coupled = coupled.reshape(ENERGIES, -1)
    part_cos = jnp.dot(cos_table, flat_coupled, preferred_element_type=jnp.float32).reshape(
        ENERGIES, atom_dev, 2, PAIR
    )
    part_sin = jnp.dot(sin_table, flat_coupled, preferred_element_type=jnp.float32).reshape(
        ENERGIES, atom_dev, 2, PAIR
    )
    time_data = jnp.stack(
        [part_cos[:, :, 0] + part_sin[:, :, 1], part_cos[:, :, 1] - part_sin[:, :, 0]], axis=2
    ).astype(jnp.bfloat16)
    own_momentum = lax.axis_index("mom")
    mode_count = phonon.shape[0]
    mode_ids = jnp.arange(mode_count, dtype=jnp.int32)
    own_modes = lax.dynamic_slice_in_dim(mode_table, own_momentum, 1, 0)[0]
    phonon_flat = phonon.reshape(mode_count, -1)
    received = lax.all_gather(time_data[None], "mom", axis=0, tiled=True)
    row_count = received.shape[0]
    one_hot = (own_modes[:, None] == mode_ids[None, :]).astype(jnp.float32)
    kernel = jnp.dot(one_hot, phonon_flat, precision=highest).reshape(row_count, 2, ENERGIES)
    values = received.astype(jnp.float32)
    kernel_re = kernel[:, 0][:, :, None, None]
    kernel_im = kernel[:, 1][:, :, None, None]
    add_re = jnp.sum(kernel_re * values[:, :, :, 0] - kernel_im * values[:, :, :, 1], axis=0)
    add_im = jnp.sum(kernel_re * values[:, :, :, 1] + kernel_im * values[:, :, :, 0], axis=0)
    summed = jnp.stack([add_re, add_im], axis=2)
    convolved = summed.astype(jnp.bfloat16)
    flat_conv = convolved.reshape(ENERGIES, -1)
    back_cos = jnp.dot(cos_table, flat_conv, preferred_element_type=jnp.float32).reshape(
        ENERGIES, atom_dev, 2, PAIR
    )
    back_sin = jnp.dot(sin_table, flat_conv, preferred_element_type=jnp.float32).reshape(
        ENERGIES, atom_dev, 2, PAIR
    )
    result_re = (back_cos[:, :, 0] - back_sin[:, :, 1]) * (1.0 / ENERGIES)
    result_im = (back_cos[:, :, 1] + back_sin[:, :, 0]) * (1.0 / ENERGIES)
    return jnp.stack([result_re, result_im], axis=2)[None].astype(jnp.bfloat16)


MESH = pl.DeviceIdType.MESH


def phase_plan(atom_dev):
    if atom_dev < 4:
        return [(start, 1) for start in range(atom_dev)]
    first = atom_dev // 2
    return [(0, first)] + [(start, 1) for start in range(first, atom_dev)]


def fused_kernel(
    phases,
    shard_count,
    mom_count,
    green_hbm,
    mixing_ref,
    occ_ref,
    target_ref,
    coupling_hbm,
    phonon_ref,
    cos_ref,
    sin_ref,
    out_ref,
    green_buf,
    full_buf,
    send_buf,
    recv_buf,
    coupling_buf,
    time_buf,
    green_sem,
    coupling_sem,
    own_sem,
    send_sem,
    recv_sem,
    mom_send_sem,
    mom_recv_sem,
):
    me = lax.axis_index("shard")
    mom = lax.axis_index("mom")
    layers, energy_dev = green_buf.shape[0], green_buf.shape[1]
    atom_dev = recv_buf.shape[0]
    dev_layer = ATL // atom_dev
    half = layers // 2
    pieces = NORB // 2
    last = len(phases) - 1

    def layer_at(step):
        home = lax.div(me, dev_layer)
        side = lax.rem(lax.div(home, half) + 1 + lax.div(step, half), 2)
        return side * half + lax.rem(home + step, half)

    def green_copy(layer):
        return pltpu.make_async_copy(
            green_hbm.at[:, layer], green_buf.at[layer], green_sem.at[layer]
        )

    def coupling_copy():
        return pltpu.make_async_copy(coupling_hbm, coupling_buf, coupling_sem)

    def own_copy(phase):
        start, size = phases[phase]
        return pltpu.make_async_copy(
            send_buf.at[pl.ds(me * atom_dev + start, size)],
            recv_buf.at[pl.ds(start, size), :, me],
            own_sem.at[phase],
        )

    def send_copy(phase, dest):
        start, size = phases[phase]
        return pltpu.make_async_remote_copy(
            src_ref=send_buf.at[pl.ds(dest * atom_dev + start, size)],
            dst_ref=recv_buf.at[pl.ds(start, size), :, me],
            send_sem=send_sem.at[phase, dest],
            recv_sem=recv_sem.at[phase, me],
            device_id={"shard": dest},
            device_id_type=MESH,
        )

    def arrive_copy(phase, source):
        start, size = phases[phase]
        return pltpu.make_async_remote_copy(
            src_ref=send_buf.at[pl.ds(source * atom_dev + start, size)],
            dst_ref=recv_buf.at[pl.ds(start, size), :, source],
            send_sem=send_sem.at[phase, source],
            recv_sem=recv_sem.at[phase, source],
            device_id={"shard": source},
            device_id_type=MESH,
        )

    def mom_copy(phase, step, sending):
        start, size = phases[phase]
        dest = lax.rem(mom + step, mom_count)
        source = lax.rem(mom + mom_count - step, mom_count)
        origin = mom if sending else source
        return pltpu.make_async_remote_copy(
            src_ref=time_buf.at[mom, pl.ds(start, size)],
            dst_ref=time_buf.at[origin, pl.ds(start, size)],
            send_sem=mom_send_sem.at[phase, step - 1],
            recv_sem=mom_recv_sem.at[phase, step - 1],
            device_id={"mom": dest},
            device_id_type=MESH,
        )

    for step in range(layers):
        green_copy(layer_at(step)).start()
    coupling_copy().start()

    barrier = pltpu.get_barrier_semaphore()
    for step in range(1, shard_count):
        pl.semaphore_signal(
            barrier,
            inc=1,
            device_id={"shard": lax.rem(me + step, shard_count)},
            device_id_type=MESH,
        )
    for step in range(1, mom_count):
        pl.semaphore_signal(
            barrier,
            inc=1,
            device_id={"mom": lax.rem(mom + step, mom_count)},
            device_id_type=MESH,
        )
    pl.semaphore_wait(barrier, shard_count + mom_count - 2)

    group = 4 if energy_dev % 4 == 0 else 1

    def layer_step(step, carry):
        layer = layer_at(step)
        green_copy(layer).wait()

        def energy_step(index, inner):
            first = index * group
            joined = [
                jnp.concatenate(
                    [green_buf[layer, first + j, 0], green_buf[layer, first + j, 1]], axis=1
                )
                for j in range(group)
            ]
            left = jnp.dot(
                jnp.concatenate(joined, axis=0),
                mixing_ref[...],
                preferred_element_type=jnp.float32,
            ).astype(jnp.bfloat16)
            for j in range(group):
                turned = jnp.concatenate(
                    [-joined[j][:, ORB:], joined[j][:, :ORB]], axis=1
                )
                full = lax.dot_general(
                    left[j * ORB : (j + 1) * ORB],
                    jnp.concatenate([joined[j], turned], axis=0),
                    (((1,), (1,)), ((), ())),
                    preferred_element_type=jnp.float32,
                )
                rows = pl.ds(pl.multiple_of((first + j) * ORB, ORB), ORB)
                full_buf[0, rows, :] = full[:, :ORB]
                full_buf[1, rows, :] = full[:, ORB:]
            return inner

        lax.fori_loop(0, energy_dev // group, energy_step, 0)

        def atom_step(slot, inner):
            atom = layer * ATL + slot
            weight = occ_ref[...]
            strips = []
            for part in range(2):
                for piece in range(pieces):
                    pair = [
                        (
                            full_buf[
                                part,
                                pl.ds(slot * NORB + 2 * piece + low, energy_dev, stride=ORB),
                                :,
                            ]
                            * weight
                        ).astype(jnp.bfloat16)
                        for low in range(2)
                    ]
                    strips.append(jnp.concatenate(pair, axis=1))
            stacked = jnp.concatenate(strips, axis=0)
            row_ids = lax.broadcasted_iota(jnp.int32, (2 * ORB, ORB), 0)
            chosen = jnp.where(row_ids == target_ref[pl.ds(atom, 1), :], 1.0, 0.0)
            picked = jnp.dot(
                stacked, chosen.astype(jnp.bfloat16), preferred_element_type=jnp.float32
            )
            send_buf[atom] = picked.astype(jnp.bfloat16).reshape(2 * pieces, energy_dev, ORB)
            return inner

        lax.fori_loop(0, ATL, atom_step, 0)
        start_sends(0, layer)
        return carry

    def start_sends(phase, layer):
        for offset in range(dev_layer):
            dest = layer * dev_layer + offset

            @pl.when(dest != me)
            def _():
                if phase > 0:
                    send_copy(phase - 1, dest).wait_send()
                send_copy(phase, dest).start()

            @pl.when(dest == me)
            def _():
                own_copy(phase).start()

    def finish(phase):
        start, size = phases[phase]
        for step in range(1, mom_count):
            mom_copy(phase, step, False).wait_recv()
        for atom in range(start, start + size):
            sums = [0.0, 0.0]
            for other in range(mom_count):
                wide_re = jnp.concatenate([phonon_ref[other, 0]] * (PAIR // ORB), axis=1)
                wide_im = jnp.concatenate([phonon_ref[other, 1]] * (PAIR // ORB), axis=1)
                time_re = time_buf[other, atom, 0].astype(jnp.float32)
                time_im = time_buf[other, atom, 1].astype(jnp.float32)
                sums[0] = sums[0] + (wide_re * time_re - wide_im * time_im)
                sums[1] = sums[1] + (wide_re * time_im + wide_im * time_re)
            conv_re = sums[0].astype(jnp.bfloat16)
            conv_im = sums[1].astype(jnp.bfloat16)
            dot = functools.partial(jnp.dot, preferred_element_type=jnp.float32)
            scale = 1.0 / cos_ref.shape[0]
            res_re = (dot(cos_ref[...], conv_re) - dot(sin_ref[...], conv_im)) * scale
            res_im = (dot(cos_ref[...], conv_im) + dot(sin_ref[...], conv_re)) * scale
            base = atom * 2 * PAIR
            out_ref[:, base : base + PAIR] = res_re.astype(jnp.bfloat16)
            out_ref[:, base + PAIR : base + 2 * PAIR] = res_im.astype(jnp.bfloat16)

    def transform(phase):
        start, size = phases[phase]

        def arrive(source, carry):
            @pl.when(source != me)
            def _():
                arrive_copy(phase, source).wait_recv()

            return carry

        lax.fori_loop(0, shard_count, arrive, 0)
        own_copy(phase).wait()
        energies = shard_count * energy_dev
        for atom in range(start, start + size):
            coupled = []
            for part in range(2):
                total = 0.0
                for piece in range(0, pieces, 2):
                    block = jnp.concatenate(
                        [
                            recv_buf[atom, part * pieces + piece + low].reshape(energies, ORB)
                            for low in range(2)
                        ],
                        axis=1,
                    )
                    total = total + jnp.dot(
                        block,
                        coupling_buf[atom, piece * ORB : (piece + 2) * ORB, :],
                        preferred_element_type=jnp.float32,
                    )
                coupled.append(total.astype(jnp.bfloat16))
            dot = functools.partial(jnp.dot, preferred_element_type=jnp.float32)
            time_re = dot(cos_ref[...], coupled[0]) + dot(sin_ref[...], coupled[1])
            time_im = dot(cos_ref[...], coupled[1]) - dot(sin_ref[...], coupled[0])
            time_buf[mom, atom, 0] = time_re.astype(jnp.bfloat16)
            time_buf[mom, atom, 1] = time_im.astype(jnp.bfloat16)
        for step in range(1, mom_count):
            mom_copy(phase, step, True).start()

    lax.fori_loop(0, layers, layer_step, 0)
    coupling_copy().wait()
    for phase in range(len(phases)):
        if phase < last:

            def more(step, carry):
                start_sends(phase + 1, layer_at(step))
                return carry

            lax.fori_loop(0, layers, more, 0)
        transform(phase)
        if phase > 0:
            finish(phase - 1)
    finish(last)

    def drain(dest, carry):
        @pl.when(dest != me)
        def _():
            send_copy(last, dest).wait_send()

        return carry

    lax.fori_loop(0, shard_count, drain, 0)
    for phase in range(len(phases)):
        for step in range(1, mom_count):
            mom_copy(phase, step, True).wait_send()


def fused(shard_count, mom_count, green_ret, broadening, occupation, neighbours, orbitals,
          coupling, phonon, mode_table):
    greens = green_ret[0]
    energy_dev = greens.shape[0]
    atom_dev = coupling.shape[0]
    energies = phonon.shape[-1]
    mixing = jnp.concatenate(
        [
            jnp.concatenate([broadening[0], broadening[1]], axis=1),
            jnp.concatenate([-broadening[1], broadening[0]], axis=1),
        ],
        axis=0,
    )
    occ = jnp.broadcast_to(occupation[0][:, None], (energy_dev, ORB))
    lane = jnp.arange(ORB, dtype=jnp.int32)
    slots = neighbours % ATL
    lane_slot = lane // NORB % NBR
    lane_atom = jnp.sum(
        jnp.where(lane_slot[None, None, :] == jnp.arange(NBR)[None, :, None], slots[:, :, None], 0),
        axis=1,
    )
    target = lane_atom * NORB + (lane % NORB + lane // (NORB * NBR) * ORB)[None, :]
    first_atom = lax.axis_index("shard") * atom_dev
    own_orbitals = lax.dynamic_slice_in_dim(orbitals, first_atom, atom_dev)
    own_neighbours = lax.dynamic_slice_in_dim(neighbours, first_atom, atom_dev)
    partner = jnp.sum(
        jnp.where(
            own_neighbours[:, :, None] == jnp.arange(ATOMS, dtype=jnp.int32)[None, None, :],
            orbitals[None, None, :],
            0,
        ),
        axis=2,
    )
    counter = jnp.arange(NORB, dtype=jnp.int32)
    within = counter[None, :] < own_orbitals[:, None]
    column = counter[None, None, :] < partner[:, :, None]
    pair_index = jnp.arange(PAIR, dtype=jnp.int32)
    final = (pair_index[None, :] // NORB < own_orbitals[:, None]) & (
        pair_index[None, :] % NORB < own_orbitals[:, None]
    )
    keep = (
        within[:, :, None, None, None]
        & column[:, None, :, :, None]
        & final[:, None, None, None, :]
    )
    ordered = coupling.reshape(atom_dev, NBR, NORB, NORB, PAIR).transpose(0, 2, 1, 3, 4)
    ordered = jnp.where(keep, ordered, jnp.zeros((), coupling.dtype))
    ordered = ordered.reshape(atom_dev, NBR * PAIR, PAIR)
    modes = lax.dynamic_slice_in_dim(mode_table, lax.axis_index("mom"), 1, 0)[0]
    mode_ids = jnp.arange(phonon.shape[0], dtype=jnp.int32)
    kernels = jnp.sum(
        jnp.where((modes[:, None] == mode_ids[None, :])[:, :, None, None], phonon[None], 0.0),
        axis=1,
    )
    kernels = jnp.broadcast_to(kernels[..., None], kernels.shape + (ORB,))
    cos_table, sin_table = dft_tables(energies)
    phases = phase_plan(atom_dev)
    count = len(phases)
    vmem = pl.BlockSpec(memory_space=pltpu.VMEM)
    hbm = pl.BlockSpec(memory_space=pl.ANY)
    dma = pltpu.SemaphoreType.DMA
    result = pl.pallas_call(
        functools.partial(fused_kernel, phases, shard_count, mom_count),
        out_shape=jax.ShapeDtypeStruct((energies, atom_dev * 2 * PAIR), jnp.bfloat16),
        in_specs=[hbm, vmem, vmem, vmem, hbm, vmem, vmem, vmem],
        out_specs=vmem,
        scratch_shapes=[
            pltpu.VMEM((LAYERS, energy_dev, 2, ORB, ORB), jnp.bfloat16),
            pltpu.VMEM((2, energy_dev * ORB, ORB), jnp.float32),
            pltpu.VMEM((ATOMS, NORB, energy_dev, ORB), jnp.bfloat16),
            pltpu.VMEM((atom_dev, NORB, shard_count, energy_dev, ORB), jnp.bfloat16),
            pltpu.VMEM((atom_dev, NBR * PAIR, PAIR), jnp.bfloat16),
            pltpu.VMEM((mom_count, atom_dev, 2, energies, PAIR), jnp.bfloat16),
            dma((LAYERS,)),
            dma,
            dma((count,)),
            dma((count, shard_count)),
            dma((count, shard_count)),
            dma((count, max(mom_count - 1, 1))),
            dma((count, max(mom_count - 1, 1))),
        ],
        compiler_params=pltpu.CompilerParams(
            collective_id=0, has_side_effects=True, vmem_limit_bytes=48 * 1024 * 1024
        ),
    )(greens, mixing, occ, target, ordered, kernels, cos_table, sin_table)
    return result.reshape(1, energies, atom_dev, 2, PAIR)


def solution(mesh):
    in_specs = (
        P("mom", "shard", None, None, None, None),
        P(),
        P("mom", "shard"),
        P(),
        P(),
        P("shard", None, None, None),
        P(),
        P(),
    )
    out_specs = P("mom", None, "shard", None, None)
    shard_count, mom_count = mesh.shape["shard"], mesh.shape["mom"]

    def body(*args):
        energy_dev, atom_dev = args[0].shape[1], args[5].shape[0]
        if energy_dev % 16 == 0 and ATL % atom_dev == 0:
            return fused(shard_count, mom_count, *args)
        return local(*args)

    return jax.shard_map(body, mesh=mesh, in_specs=in_specs, out_specs=out_specs, check_vma=False)
```

```python
import functools
import math

import jax
import jax.numpy as jnp
import numpy as np
from jax import lax
from jax.experimental import pallas as pl
from jax.experimental.pallas import tpu as pltpu
from jax.sharding import PartitionSpec as P

NORB = 16
ATL = 8
NBR = 4
ENERGIES = 256
LAYERS = 8
ORB = 128
PAIR = 256
ATOMS = 64


def dft_tables(length):
    counter = jnp.arange(length, dtype=jnp.int32)
    phases = counter[:, None] * counter[None, :] % length
    angles = phases.astype(jnp.float32) * (2.0 * math.pi / length)
    return (jnp.cos(angles).astype(jnp.bfloat16), jnp.sin(angles).astype(jnp.bfloat16))


def local(green_ret, broadening, occupation, neighbours, orbitals, coupling, phonon, mode_table):
    highest = lax.Precision.HIGHEST
    greens = green_ret[0]
    energy_dev = greens.shape[0]
    mixing = jnp.stack(
        [
            jnp.concatenate([broadening[0], broadening[1]], axis=1),
            jnp.concatenate([-broadening[1], broadening[0]], axis=1),
        ],
        axis=0,
    )
    left = jnp.einsum("elpik,pkq->eliq", greens, mixing, preferred_element_type=jnp.float32).astype(
        jnp.bfloat16
    )
    slot_atoms = neighbours % ATL
    selector = slot_atoms[:, :, None] == jnp.arange(ATL, dtype=jnp.int32)[None, None, :]
    layer_orbitals = jnp.repeat(orbitals.reshape(LAYERS, ATL), ATL, axis=0)
    partner_count = jnp.sum(jnp.where(selector, layer_orbitals[:, None, :], 0), axis=2)
    green_rows = greens.reshape(energy_dev, LAYERS, 2, ATL, NORB, ORB)
    select_bf = selector.reshape(LAYERS, ATL, NBR, ATL).astype(jnp.bfloat16)
    partner_rows = jnp.einsum(
        "ljnm,elpmic->eljnpic", select_bf, green_rows, preferred_element_type=jnp.float32
    ).astype(jnp.bfloat16)
    partner_re = partner_rows[:, :, :, :, 0]
    partner_im = partner_rows[:, :, :, :, 1]
    left_rows_re = left[..., :ORB].reshape(energy_dev, LAYERS, ATL, NORB, ORB)
    left_rows_im = left[..., ORB:].reshape(energy_dev, LAYERS, ATL, NORB, ORB)
    pair_re = jnp.einsum(
        "eljic,eljnkc->eljnik", left_rows_re, partner_re, preferred_element_type=jnp.float32
    ) + jnp.einsum(
        "eljic,eljnkc->eljnik", left_rows_im, partner_im, preferred_element_type=jnp.float32
    )
    pair_im = jnp.einsum(
        "eljic,eljnkc->eljnik", left_rows_im, partner_re, preferred_element_type=jnp.float32
    ) - jnp.einsum(
        "eljic,eljnkc->eljnik", left_rows_re, partner_im, preferred_element_type=jnp.float32
    )
    chosen = jnp.stack([pair_re, pair_im], axis=4)
    chosen = chosen.reshape(energy_dev, ATOMS, NBR, 2, NORB, NORB)
    counter = jnp.arange(NORB, dtype=jnp.int32)
    row_mask = counter[None, :] < orbitals[:, None]
    column_mask = counter[None, None, :] < partner_count[:, :, None]
    pair_mask = (row_mask[:, None, :, None] & column_mask[:, :, None, :]).astype(jnp.float32)
    scaled = (
        chosen * occupation[0][:, None, None, None, None, None] * pair_mask[None, :, :, None, :, :]
    )
    pair_blocks = scaled.reshape(energy_dev, ATOMS, NBR, 2, PAIR).astype(jnp.bfloat16)
    arrived = lax.all_to_all(pair_blocks, "shard", split_axis=1, concat_axis=0, tiled=True)
    atom_dev = arrived.shape[1]
    mixed_terms = jnp.einsum(
        "eanpx,anxy->eapy", arrived, coupling, preferred_element_type=jnp.float32
    )
    first_atom = lax.axis_index("shard") * atom_dev
    own_orbitals = lax.dynamic_slice_in_dim(orbitals, first_atom, atom_dev)
    pair_index = jnp.arange(PAIR, dtype=jnp.int32)
    own_mask = (
        (pair_index[None, :] // NORB < own_orbitals[:, None])
        & (pair_index[None, :] % NORB < own_orbitals[:, None])
    ).astype(jnp.float32)
    coupled = (mixed_terms * own_mask[None, :, None, :]).astype(jnp.bfloat16)
    cos_table, sin_table = dft_tables(ENERGIES)
    flat_coupled = coupled.reshape(ENERGIES, -1)
    part_cos = jnp.dot(cos_table, flat_coupled, preferred_element_type=jnp.float32).reshape(
        ENERGIES, atom_dev, 2, PAIR
    )
    part_sin = jnp.dot(sin_table, flat_coupled, preferred_element_type=jnp.float32).reshape(
        ENERGIES, atom_dev, 2, PAIR
    )
    time_data = jnp.stack(
        [part_cos[:, :, 0] + part_sin[:, :, 1], part_cos[:, :, 1] - part_sin[:, :, 0]], axis=2
    ).astype(jnp.bfloat16)
    own_momentum = lax.axis_index("mom")
    mode_count = phonon.shape[0]
    mode_ids = jnp.arange(mode_count, dtype=jnp.int32)
    own_modes = lax.dynamic_slice_in_dim(mode_table, own_momentum, 1, 0)[0]
    phonon_flat = phonon.reshape(mode_count, -1)
    received = lax.all_gather(time_data[None], "mom", axis=0, tiled=True)
    row_count = received.shape[0]
    one_hot = (own_modes[:, None] == mode_ids[None, :]).astype(jnp.float32)
    kernel = jnp.dot(one_hot, phonon_flat, precision=highest).reshape(row_count, 2, ENERGIES)
    values = received.astype(jnp.float32)
    kernel_re = kernel[:, 0][:, :, None, None]
    kernel_im = kernel[:, 1][:, :, None, None]
    add_re = jnp.sum(kernel_re * values[:, :, :, 0] - kernel_im * values[:, :, :, 1], axis=0)
    add_im = jnp.sum(kernel_re * values[:, :, :, 1] + kernel_im * values[:, :, :, 0], axis=0)
    summed = jnp.stack([add_re, add_im], axis=2)
    convolved = summed.astype(jnp.bfloat16)
    flat_conv = convolved.reshape(ENERGIES, -1)
    back_cos = jnp.dot(cos_table, flat_conv, preferred_element_type=jnp.float32).reshape(
        ENERGIES, atom_dev, 2, PAIR
    )
    back_sin = jnp.dot(sin_table, flat_conv, preferred_element_type=jnp.float32).reshape(
        ENERGIES, atom_dev, 2, PAIR
    )
    result_re = (back_cos[:, :, 0] - back_sin[:, :, 1]) * (1.0 / ENERGIES)
    result_im = (back_cos[:, :, 1] + back_sin[:, :, 0]) * (1.0 / ENERGIES)
    return jnp.stack([result_re, result_im], axis=2)[None].astype(jnp.bfloat16)


MESH = pl.DeviceIdType.MESH


def phase_plan(atom_dev):
    if atom_dev < 2:
        return [(0, atom_dev)]
    return [(0, atom_dev - 1), (atom_dev - 1, 1)]


def fused_kernel(
    phases,
    shard_count,
    mom_count,
    green_hbm,
    broadening_ref,
    occupation_ref,
    neighbours_ref,
    orbitals_ref,
    coupling_hbm,
    phonon_ref,
    modes_ref,
    cos_ref,
    sin_ref,
    out_ref,
    green_buf,
    full_buf,
    send_buf,
    recv_buf,
    coupling_buf,
    kernel_buf,
    mixing_ref,
    time_buf,
    green_sem,
    coupling_sem,
    own_sem,
    send_sem,
    recv_sem,
    mom_send_sem,
    mom_recv_sem,
):
    me = lax.axis_index("shard")
    mom = lax.axis_index("mom")
    layers, energy_dev = green_buf.shape[0], green_buf.shape[1]
    atom_dev = recv_buf.shape[0]
    dev_layer = ATL // atom_dev
    half = layers // 2
    pieces = NORB // 2
    last = len(phases) - 1

    def layer_at(step):
        home = lax.div(me, dev_layer)
        side = lax.rem(lax.div(home, half) + 1 + lax.div(step, half), 2)
        return side * half + lax.rem(home + step, half)

    def green_copy(layer):
        return pltpu.make_async_copy(
            green_hbm.at[:, layer], green_buf.at[layer], green_sem.at[layer]
        )

    def coupling_copy(slot):
        return pltpu.make_async_copy(
            coupling_hbm.at[:, slot], coupling_buf.at[:, :, slot], coupling_sem.at[slot]
        )

    def own_copy(phase):
        start, size = phases[phase]
        return pltpu.make_async_copy(
            send_buf.at[pl.ds(me * atom_dev + start, size)],
            recv_buf.at[pl.ds(start, size), me],
            own_sem.at[phase],
        )

    def send_copy(phase, dest):
        start, size = phases[phase]
        return pltpu.make_async_remote_copy(
            src_ref=send_buf.at[pl.ds(dest * atom_dev + start, size)],
            dst_ref=recv_buf.at[pl.ds(start, size), me],
            send_sem=send_sem.at[phase, dest],
            recv_sem=recv_sem.at[phase, me],
            device_id={"shard": dest},
            device_id_type=MESH,
        )

    def arrive_copy(phase, source):
        start, size = phases[phase]
        return pltpu.make_async_remote_copy(
            src_ref=send_buf.at[pl.ds(source * atom_dev + start, size)],
            dst_ref=recv_buf.at[pl.ds(start, size), source],
            send_sem=send_sem.at[phase, source],
            recv_sem=recv_sem.at[phase, source],
            device_id={"shard": source},
            device_id_type=MESH,
        )

    def mom_copy(phase, step, sending):
        start, size = phases[phase]
        dest = lax.rem(mom + step, mom_count)
        source = lax.rem(mom + mom_count - step, mom_count)
        origin = mom if sending else source
        return pltpu.make_async_remote_copy(
            src_ref=time_buf.at[mom, pl.ds(start, size)],
            dst_ref=time_buf.at[origin, pl.ds(start, size)],
            send_sem=mom_send_sem.at[phase, step - 1],
            recv_sem=mom_recv_sem.at[phase, step - 1],
            device_id={"mom": dest},
            device_id_type=MESH,
        )

    for step in range(layers):
        green_copy(layer_at(step)).start()
    for slot in range(NBR):
        coupling_copy(slot).start()

    barrier = pltpu.get_barrier_semaphore()
    for step in range(1, shard_count):
        pl.semaphore_signal(
            barrier,
            inc=1,
            device_id={"shard": lax.rem(me + step, shard_count)},
            device_id_type=MESH,
        )
    for step in range(1, mom_count):
        pl.semaphore_signal(
            barrier,
            inc=1,
            device_id={"mom": lax.rem(mom + step, mom_count)},
            device_id_type=MESH,
        )
    mixing_ref[:ORB, :ORB] = broadening_ref[0]
    mixing_ref[:ORB, ORB:] = broadening_ref[1]
    mixing_ref[ORB:, :ORB] = -broadening_ref[1]
    mixing_ref[ORB:, ORB:] = broadening_ref[0]
    group = 8
    unroll = 4

    def layer_pairs(layer):
        green_copy(layer).wait()

        def energy_step(index, inner):
            first = index * group
            joined = [
                jnp.concatenate(
                    [green_buf[layer, first + j, 0], green_buf[layer, first + j, 1]], axis=1
                )
                for j in range(group)
            ]
            left = jnp.dot(
                jnp.concatenate(joined, axis=0),
                mixing_ref[...],
                preferred_element_type=jnp.float32,
            ).astype(jnp.bfloat16)
            for j in range(group):
                turned = jnp.concatenate(
                    [-joined[j][:, ORB:], joined[j][:, :ORB]], axis=1
                )
                full = lax.dot_general(
                    left[j * ORB : (j + 1) * ORB],
                    jnp.concatenate([joined[j], turned], axis=0),
                    (((1,), (1,)), ((), ())),
                    preferred_element_type=jnp.float32,
                )
                full = full * occupation_ref[0, first + j]
                rows = pl.ds(pl.multiple_of((first + j) * ORB, ORB), ORB)
                full_buf[0, rows, :] = full[:, :ORB]
                full_buf[1, rows, :] = full[:, ORB:]
            return inner

        lax.fori_loop(0, energy_dev // group, energy_step, 0)

        lane = lax.broadcasted_iota(jnp.int32, (1, ORB), 1)
        lane_slot = lax.rem(lax.div(lane, NORB), NBR)
        lane_base = lax.rem(lane, NORB) + lax.div(lane, NORB * NBR) * ORB
        row_ids = lax.broadcasted_iota(jnp.int32, (2 * ORB, ORB), 0)

        def pick_atom(slot):
            atom = layer * ATL + slot
            target = lane_base
            for near in range(NBR):
                start = (neighbours_ref[atom, near] - layer * ATL) * NORB
                target = target + jnp.where(lane_slot == near, start, 0)
            strips = []
            for part in range(2):
                for piece in range(pieces):
                    pair = [
                        full_buf[
                            part,
                            pl.ds(slot * NORB + 2 * piece + low, energy_dev, stride=ORB),
                            :,
                        ].astype(jnp.bfloat16)
                        for low in range(2)
                    ]
                    strips.append(jnp.concatenate(pair, axis=1))
            stacked = jnp.concatenate(strips, axis=0)
            chosen = jnp.where(row_ids == target, 1.0, 0.0)
            picked = jnp.dot(
                stacked, chosen.astype(jnp.bfloat16), preferred_element_type=jnp.float32
            )
            send_buf[atom] = picked.astype(jnp.bfloat16).reshape(2 * pieces, energy_dev, ORB)

        def atom_step(index, inner):
            for j in range(unroll):
                pick_atom(index * unroll + j)
            return inner

        lax.fori_loop(0, ATL // unroll, atom_step, 0)

    def layer_step(step, carry):
        layer_pairs(layer_at(step))
        start_sends(0, layer_at(step))
        return carry

    def mask_coupling():
        shape = (NORB, PAIR)
        column = lax.broadcasted_iota(jnp.int32, shape, 0)
        entry = lax.broadcasted_iota(jnp.int32, shape, 1)
        outer, inner = lax.div(entry, NORB), lax.rem(entry, NORB)
        for slot in range(NBR):
            coupling_copy(slot).wait()
        for atom in range(atom_dev):
            place = me * atom_dev + atom
            own = orbitals_ref[place]
            kept = (outer < own) & (inner < own)
            masks = [
                jnp.where(kept & (column < orbitals_ref[neighbours_ref[place, near]]), 1.0, 0.0)
                for near in range(NBR)
            ]

            def row_step(row, carry):
                used = jnp.where(row < own, 1.0, 0.0)
                for near in range(NBR):
                    block = coupling_buf[atom, row, near].astype(jnp.float32)
                    coupling_buf[atom, row, near] = (block * (masks[near] * used)).astype(
                        jnp.bfloat16
                    )
                return carry

            lax.fori_loop(0, NORB, row_step, 0)

    def spread_phonon():
        for other in range(mom_count):
            mode = modes_ref[mom, other]
            rows = phonon_ref[mode]
            for part in range(2):
                wide = jnp.broadcast_to(rows[part : part + 1], (ORB, rows.shape[1]))
                kernel_buf[other, part] = wide.T

    def start_sends(phase, layer):
        for offset in range(dev_layer):
            dest = layer * dev_layer + offset

            @pl.when(dest != me)
            def _():
                if phase > 0:
                    send_copy(phase - 1, dest).wait_send()
                send_copy(phase, dest).start()

            @pl.when(dest == me)
            def _():
                own_copy(phase).start()

    def finish(phase):
        start, size = phases[phase]
        for step in range(1, mom_count):
            mom_copy(phase, step, False).wait_recv()
        for atom in range(start, start + size):
            sums = [0.0, 0.0]
            for other in range(mom_count):
                wide_re = jnp.concatenate([kernel_buf[other, 0]] * (PAIR // ORB), axis=1)
                wide_im = jnp.concatenate([kernel_buf[other, 1]] * (PAIR // ORB), axis=1)
                time_re = time_buf[other, atom, 0].astype(jnp.float32)
                time_im = time_buf[other, atom, 1].astype(jnp.float32)
                sums[0] = sums[0] + (wide_re * time_re - wide_im * time_im)
                sums[1] = sums[1] + (wide_re * time_im + wide_im * time_re)
            conv_re = sums[0].astype(jnp.bfloat16)
            conv_im = sums[1].astype(jnp.bfloat16)
            dot = functools.partial(jnp.dot, preferred_element_type=jnp.float32)
            scale = 1.0 / cos_ref.shape[0]
            res_re = (dot(cos_ref[...], conv_re) - dot(sin_ref[...], conv_im)) * scale
            res_im = (dot(cos_ref[...], conv_im) + dot(sin_ref[...], conv_re)) * scale
            base = atom * 2 * PAIR
            out_ref[:, base : base + PAIR] = res_re.astype(jnp.bfloat16)
            out_ref[:, base + PAIR : base + 2 * PAIR] = res_im.astype(jnp.bfloat16)

    def transform(phase):
        start, size = phases[phase]

        def arrive(source, carry):
            @pl.when(source != me)
            def _():
                arrive_copy(phase, source).wait_recv()

            return carry

        lax.fori_loop(0, shard_count, arrive, 0)
        own_copy(phase).wait()
        energies = shard_count * energy_dev
        for atom in range(start, start + size):
            coupled = []
            for part in range(2):
                total = 0.0
                for piece in range(0, pieces, 2):
                    block = jnp.concatenate(
                        [
                            recv_buf[atom, :, part * pieces + piece + low].reshape(energies, ORB)
                            for low in range(2)
                        ],
                        axis=1,
                    )
                    total = total + jnp.dot(
                        block,
                        coupling_buf[atom, 2 * piece : 2 * piece + 4].reshape(PAIR, PAIR),
                        preferred_element_type=jnp.float32,
                    )
                coupled.append(total.astype(jnp.bfloat16))
            dot = functools.partial(jnp.dot, preferred_element_type=jnp.float32)
            time_re = dot(cos_ref[...], coupled[0]) + dot(sin_ref[...], coupled[1])
            time_im = dot(cos_ref[...], coupled[1]) - dot(sin_ref[...], coupled[0])
            time_buf[mom, atom, 0] = time_re.astype(jnp.bfloat16)
            time_buf[mom, atom, 1] = time_im.astype(jnp.bfloat16)
        for step in range(1, mom_count):
            mom_copy(phase, step, True).start()

    layer_pairs(layer_at(0))
    pl.semaphore_wait(barrier, shard_count + mom_count - 2)
    start_sends(0, layer_at(0))
    lax.fori_loop(1, layers, layer_step, 0)
    mask_coupling()
    spread_phonon()
    for phase in range(len(phases)):
        if phase < last:

            def more(step, carry):
                start_sends(phase + 1, layer_at(step))
                return carry

            lax.fori_loop(0, layers, more, 0)
        transform(phase)
        if phase > 0:
            finish(phase - 1)
    finish(last)

    def drain(dest, carry):
        @pl.when(dest != me)
        def _():
            send_copy(last, dest).wait_send()

        return carry

    lax.fori_loop(0, shard_count, drain, 0)
    for phase in range(len(phases)):
        for step in range(1, mom_count):
            mom_copy(phase, step, True).wait_send()


def fused(shard_count, mom_count, green_ret, broadening, occupation, neighbours, orbitals,
          coupling, phonon, mode_table):
    greens = green_ret[0]
    energy_dev = greens.shape[0]
    atom_dev = coupling.shape[0]
    energies = phonon.shape[-1]
    counter = np.arange(energies, dtype=np.int32)
    angles = (counter[:, None] * counter[None, :] % energies).astype(np.float32)
    angles = angles * np.float32(2.0 * math.pi / energies)
    cos_table = jnp.asarray(np.cos(angles), jnp.bfloat16)
    sin_table = jnp.asarray(np.sin(angles), jnp.bfloat16)
    blocks = coupling.reshape(atom_dev, NBR, NORB, NORB, PAIR)
    phases = phase_plan(atom_dev)
    count = len(phases)
    vmem = pl.BlockSpec(memory_space=pltpu.VMEM)
    hbm = pl.BlockSpec(memory_space=pl.ANY)
    smem = pl.BlockSpec(memory_space=pltpu.SMEM)
    dma = pltpu.SemaphoreType.DMA
    result = pl.pallas_call(
        functools.partial(fused_kernel, phases, shard_count, mom_count),
        out_shape=jax.ShapeDtypeStruct((energies, atom_dev * 2 * PAIR), jnp.bfloat16),
        in_specs=[hbm, vmem, smem, smem, smem, hbm, vmem, smem, vmem, vmem],
        out_specs=vmem,
        scratch_shapes=[
            pltpu.VMEM((LAYERS, energy_dev, 2, ORB, ORB), jnp.bfloat16),
            pltpu.VMEM((2, energy_dev * ORB, ORB), jnp.float32),
            pltpu.VMEM((ATOMS, NORB, energy_dev, ORB), jnp.bfloat16),
            pltpu.VMEM((atom_dev, shard_count, NORB, energy_dev, ORB), jnp.bfloat16),
            pltpu.VMEM((atom_dev, NORB, NBR, NORB, PAIR), jnp.bfloat16),
            pltpu.VMEM((mom_count, 2, energies, ORB), jnp.float32),
            pltpu.VMEM((2 * ORB, 2 * ORB), jnp.bfloat16),
            pltpu.VMEM((mom_count, atom_dev, 2, energies, PAIR), jnp.bfloat16),
            dma((LAYERS,)),
            dma((NBR,)),
            dma((count,)),
            dma((count, shard_count)),
            dma((count, shard_count)),
            dma((count, max(mom_count - 1, 1))),
            dma((count, max(mom_count - 1, 1))),
        ],
        compiler_params=pltpu.CompilerParams(
            collective_id=0, has_side_effects=True, vmem_limit_bytes=48 * 1024 * 1024
        ),
    )(
        greens, broadening, occupation, neighbours, orbitals, blocks, phonon, mode_table,
        cos_table, sin_table,
    )
    return result.reshape(1, energies, atom_dev, 2, PAIR)


def solution(mesh):
    in_specs = (
        P("mom", "shard", None, None, None, None),
        P(),
        P("mom", "shard"),
        P(),
        P(),
        P("shard", None, None, None),
        P(),
        P(),
    )
    out_specs = P("mom", None, "shard", None, None)
    shard_count, mom_count = mesh.shape["shard"], mesh.shape["mom"]

    def body(*args):
        energy_dev, atom_dev = args[0].shape[1], args[5].shape[0]
        if energy_dev % 16 == 0 and ATL % atom_dev == 0:
            return fused(shard_count, mom_count, *args)
        return local(*args)

    return jax.shard_map(body, mesh=mesh, in_specs=in_specs, out_specs=out_specs, check_vma=False)
```

```python
import functools
import math

import jax
import jax.numpy as jnp
import numpy as np
from jax import lax
from jax.experimental import pallas as pl
from jax.experimental.pallas import tpu as pltpu
from jax.sharding import PartitionSpec as P

NORB = 16
ATL = 8
NBR = 4
ENERGIES = 256
LAYERS = 8
ORB = 128
PAIR = 256
ATOMS = 64


def dft_tables(length):
    counter = jnp.arange(length, dtype=jnp.int32)
    phases = counter[:, None] * counter[None, :] % length
    angles = phases.astype(jnp.float32) * (2.0 * math.pi / length)
    return (jnp.cos(angles).astype(jnp.bfloat16), jnp.sin(angles).astype(jnp.bfloat16))


def local(green_ret, broadening, occupation, neighbours, orbitals, coupling, phonon, mode_table):
    highest = lax.Precision.HIGHEST
    greens = green_ret[0]
    energy_dev = greens.shape[0]
    mixing = jnp.stack(
        [
            jnp.concatenate([broadening[0], broadening[1]], axis=1),
            jnp.concatenate([-broadening[1], broadening[0]], axis=1),
        ],
        axis=0,
    )
    left = jnp.einsum("elpik,pkq->eliq", greens, mixing, preferred_element_type=jnp.float32).astype(
        jnp.bfloat16
    )
    slot_atoms = neighbours % ATL
    selector = slot_atoms[:, :, None] == jnp.arange(ATL, dtype=jnp.int32)[None, None, :]
    layer_orbitals = jnp.repeat(orbitals.reshape(LAYERS, ATL), ATL, axis=0)
    partner_count = jnp.sum(jnp.where(selector, layer_orbitals[:, None, :], 0), axis=2)
    green_rows = greens.reshape(energy_dev, LAYERS, 2, ATL, NORB, ORB)
    select_bf = selector.reshape(LAYERS, ATL, NBR, ATL).astype(jnp.bfloat16)
    partner_rows = jnp.einsum(
        "ljnm,elpmic->eljnpic", select_bf, green_rows, preferred_element_type=jnp.float32
    ).astype(jnp.bfloat16)
    partner_re = partner_rows[:, :, :, :, 0]
    partner_im = partner_rows[:, :, :, :, 1]
    left_rows_re = left[..., :ORB].reshape(energy_dev, LAYERS, ATL, NORB, ORB)
    left_rows_im = left[..., ORB:].reshape(energy_dev, LAYERS, ATL, NORB, ORB)
    pair_re = jnp.einsum(
        "eljic,eljnkc->eljnik", left_rows_re, partner_re, preferred_element_type=jnp.float32
    ) + jnp.einsum(
        "eljic,eljnkc->eljnik", left_rows_im, partner_im, preferred_element_type=jnp.float32
    )
    pair_im = jnp.einsum(
        "eljic,eljnkc->eljnik", left_rows_im, partner_re, preferred_element_type=jnp.float32
    ) - jnp.einsum(
        "eljic,eljnkc->eljnik", left_rows_re, partner_im, preferred_element_type=jnp.float32
    )
    chosen = jnp.stack([pair_re, pair_im], axis=4)
    chosen = chosen.reshape(energy_dev, ATOMS, NBR, 2, NORB, NORB)
    counter = jnp.arange(NORB, dtype=jnp.int32)
    row_mask = counter[None, :] < orbitals[:, None]
    column_mask = counter[None, None, :] < partner_count[:, :, None]
    pair_mask = (row_mask[:, None, :, None] & column_mask[:, :, None, :]).astype(jnp.float32)
    scaled = (
        chosen * occupation[0][:, None, None, None, None, None] * pair_mask[None, :, :, None, :, :]
    )
    pair_blocks = scaled.reshape(energy_dev, ATOMS, NBR, 2, PAIR).astype(jnp.bfloat16)
    arrived = lax.all_to_all(pair_blocks, "shard", split_axis=1, concat_axis=0, tiled=True)
    atom_dev = arrived.shape[1]
    mixed_terms = jnp.einsum(
        "eanpx,anxy->eapy", arrived, coupling, preferred_element_type=jnp.float32
    )
    first_atom = lax.axis_index("shard") * atom_dev
    own_orbitals = lax.dynamic_slice_in_dim(orbitals, first_atom, atom_dev)
    pair_index = jnp.arange(PAIR, dtype=jnp.int32)
    own_mask = (
        (pair_index[None, :] // NORB < own_orbitals[:, None])
        & (pair_index[None, :] % NORB < own_orbitals[:, None])
    ).astype(jnp.float32)
    coupled = (mixed_terms * own_mask[None, :, None, :]).astype(jnp.bfloat16)
    cos_table, sin_table = dft_tables(ENERGIES)
    flat_coupled = coupled.reshape(ENERGIES, -1)
    part_cos = jnp.dot(cos_table, flat_coupled, preferred_element_type=jnp.float32).reshape(
        ENERGIES, atom_dev, 2, PAIR
    )
    part_sin = jnp.dot(sin_table, flat_coupled, preferred_element_type=jnp.float32).reshape(
        ENERGIES, atom_dev, 2, PAIR
    )
    time_data = jnp.stack(
        [part_cos[:, :, 0] + part_sin[:, :, 1], part_cos[:, :, 1] - part_sin[:, :, 0]], axis=2
    ).astype(jnp.bfloat16)
    own_momentum = lax.axis_index("mom")
    mode_count = phonon.shape[0]
    mode_ids = jnp.arange(mode_count, dtype=jnp.int32)
    own_modes = lax.dynamic_slice_in_dim(mode_table, own_momentum, 1, 0)[0]
    phonon_flat = phonon.reshape(mode_count, -1)
    received = lax.all_gather(time_data[None], "mom", axis=0, tiled=True)
    row_count = received.shape[0]
    one_hot = (own_modes[:, None] == mode_ids[None, :]).astype(jnp.float32)
    kernel = jnp.dot(one_hot, phonon_flat, precision=highest).reshape(row_count, 2, ENERGIES)
    values = received.astype(jnp.float32)
    kernel_re = kernel[:, 0][:, :, None, None]
    kernel_im = kernel[:, 1][:, :, None, None]
    add_re = jnp.sum(kernel_re * values[:, :, :, 0] - kernel_im * values[:, :, :, 1], axis=0)
    add_im = jnp.sum(kernel_re * values[:, :, :, 1] + kernel_im * values[:, :, :, 0], axis=0)
    summed = jnp.stack([add_re, add_im], axis=2)
    convolved = summed.astype(jnp.bfloat16)
    flat_conv = convolved.reshape(ENERGIES, -1)
    back_cos = jnp.dot(cos_table, flat_conv, preferred_element_type=jnp.float32).reshape(
        ENERGIES, atom_dev, 2, PAIR
    )
    back_sin = jnp.dot(sin_table, flat_conv, preferred_element_type=jnp.float32).reshape(
        ENERGIES, atom_dev, 2, PAIR
    )
    result_re = (back_cos[:, :, 0] - back_sin[:, :, 1]) * (1.0 / ENERGIES)
    result_im = (back_cos[:, :, 1] + back_sin[:, :, 0]) * (1.0 / ENERGIES)
    return jnp.stack([result_re, result_im], axis=2)[None].astype(jnp.bfloat16)


MESH = pl.DeviceIdType.MESH


def phase_plan(atom_dev):
    if atom_dev < 4:
        return [(start, 1) for start in range(atom_dev)]
    first = atom_dev // 2
    return [(0, first)] + [(start, 1) for start in range(first, atom_dev)]


def fused_kernel(
    phases,
    shard_count,
    mom_count,
    green_hbm,
    broadening_hbm,
    occupation_hbm,
    neighbours_hbm,
    orbitals_hbm,
    coupling_hbm,
    phonon_hbm,
    modes_hbm,
    cos_hbm,
    sin_hbm,
    out_ref,
    broadening_ref,
    occupation_ref,
    neighbours_ref,
    orbitals_ref,
    phonon_ref,
    modes_ref,
    cos_ref,
    sin_ref,
    small_sem,
    green_buf,
    full_buf,
    send_buf,
    recv_buf,
    coupling_buf,
    kernel_buf,
    mixing_ref,
    time_buf,
    green_sem,
    coupling_sem,
    own_sem,
    send_sem,
    recv_sem,
    mom_send_sem,
    mom_recv_sem,
):
    me = lax.axis_index("shard")
    mom = lax.axis_index("mom")
    layers, energy_dev = green_buf.shape[0], green_buf.shape[1]
    atom_dev = recv_buf.shape[0]
    dev_layer = ATL // atom_dev
    half = layers // 2
    pieces = NORB // 2
    last = len(phases) - 1
    early = min(2, len(phases))

    def layer_at(step):
        home = lax.div(me, dev_layer)
        side = lax.rem(lax.div(home, half) + 1 + step, 2)
        return side * half + lax.rem(home + lax.div(step, 2), half)

    def green_copy(layer):
        return pltpu.make_async_copy(
            green_hbm.at[:, layer], green_buf.at[layer], green_sem.at[layer]
        )

    def coupling_copy(slot):
        return pltpu.make_async_copy(
            coupling_hbm.at[:, slot], coupling_buf.at[:, :, slot], coupling_sem.at[slot]
        )

    def own_copy(phase):
        start, size = phases[phase]
        return pltpu.make_async_copy(
            send_buf.at[pl.ds(me * atom_dev + start, size)],
            recv_buf.at[pl.ds(start, size), me],
            own_sem.at[phase],
        )

    def send_copy(phase, dest):
        start, size = phases[phase]
        return pltpu.make_async_remote_copy(
            src_ref=send_buf.at[pl.ds(dest * atom_dev + start, size)],
            dst_ref=recv_buf.at[pl.ds(start, size), me],
            send_sem=send_sem.at[phase, dest],
            recv_sem=recv_sem.at[phase, me],
            device_id={"shard": dest},
            device_id_type=MESH,
        )

    def arrive_copy(phase, source):
        start, size = phases[phase]
        return pltpu.make_async_remote_copy(
            src_ref=send_buf.at[pl.ds(source * atom_dev + start, size)],
            dst_ref=recv_buf.at[pl.ds(start, size), source],
            send_sem=send_sem.at[phase, source],
            recv_sem=recv_sem.at[phase, source],
            device_id={"shard": source},
            device_id_type=MESH,
        )

    def mom_copy(phase, step, sending):
        start, size = phases[phase]
        dest = lax.rem(mom + step, mom_count)
        source = lax.rem(mom + mom_count - step, mom_count)
        origin = mom if sending else source
        return pltpu.make_async_remote_copy(
            src_ref=time_buf.at[mom, pl.ds(start, size)],
            dst_ref=time_buf.at[origin, pl.ds(start, size)],
            send_sem=mom_send_sem.at[phase, step - 1],
            recv_sem=mom_recv_sem.at[phase, step - 1],
            device_id={"mom": dest},
            device_id_type=MESH,
        )

    small = [
        (broadening_hbm, broadening_ref),
        (occupation_hbm, occupation_ref),
        (neighbours_hbm, neighbours_ref),
        (orbitals_hbm, orbitals_ref),
        (phonon_hbm, phonon_ref),
        (modes_hbm, modes_ref),
        (cos_hbm, cos_ref),
        (sin_hbm, sin_ref),
    ]
    small = [
        pltpu.make_async_copy(source, held, small_sem.at[index])
        for index, (source, held) in enumerate(small)
    ]
    for copy in small[:4]:
        copy.start()
    for step in range(layers):
        green_copy(layer_at(step)).start()
    for copy in small[4:]:
        copy.start()
    for slot in range(NBR):
        coupling_copy(slot).start()

    barrier = pltpu.get_barrier_semaphore()
    for step in range(1, shard_count):
        pl.semaphore_signal(
            barrier,
            inc=1,
            device_id={"shard": lax.rem(me + step, shard_count)},
            device_id_type=MESH,
        )
    for step in range(1, mom_count):
        pl.semaphore_signal(
            barrier,
            inc=1,
            device_id={"mom": lax.rem(mom + step, mom_count)},
            device_id_type=MESH,
        )
    for copy in small[:4]:
        copy.wait()
    mixing_ref[:ORB, :ORB] = broadening_ref[0]
    mixing_ref[:ORB, ORB:] = broadening_ref[1]
    mixing_ref[ORB:, :ORB] = -broadening_ref[1]
    mixing_ref[ORB:, ORB:] = broadening_ref[0]
    group = 8
    unroll = 4

    def layer_pairs(layer):
        green_copy(layer).wait()

        def energy_step(index, inner):
            first = index * group
            joined = [
                jnp.concatenate(
                    [green_buf[layer, first + j, 0], green_buf[layer, first + j, 1]], axis=1
                )
                for j in range(group)
            ]
            left = jnp.dot(
                jnp.concatenate(joined, axis=0),
                mixing_ref[...],
                preferred_element_type=jnp.float32,
            ).astype(jnp.bfloat16)
            for j in range(group):
                turned = jnp.concatenate(
                    [-joined[j][:, ORB:], joined[j][:, :ORB]], axis=1
                )
                full = lax.dot_general(
                    left[j * ORB : (j + 1) * ORB],
                    jnp.concatenate([joined[j], turned], axis=0),
                    (((1,), (1,)), ((), ())),
                    preferred_element_type=jnp.float32,
                )
                full = full * occupation_ref[0, first + j]
                rows = pl.ds(pl.multiple_of((first + j) * ORB, ORB), ORB)
                full_buf[0, rows, :] = full[:, :ORB]
                full_buf[1, rows, :] = full[:, ORB:]
            return inner

        lax.fori_loop(0, energy_dev // group, energy_step, 0)

        lane = lax.broadcasted_iota(jnp.int32, (1, ORB), 1)
        lane_slot = lax.rem(lax.div(lane, NORB), NBR)
        lane_base = lax.rem(lane, NORB) + lax.div(lane, NORB * NBR) * ORB
        row_ids = lax.broadcasted_iota(jnp.int32, (2 * ORB, ORB), 0)

        def pick_atom(slot):
            atom = layer * ATL + slot
            target = lane_base
            for near in range(NBR):
                start = (neighbours_ref[near, atom] - layer * ATL) * NORB
                target = target + jnp.where(lane_slot == near, start, 0)
            strips = []
            for part in range(2):
                for piece in range(pieces):
                    pair = [
                        full_buf[
                            part,
                            pl.ds(slot * NORB + 2 * piece + low, energy_dev, stride=ORB),
                            :,
                        ].astype(jnp.bfloat16)
                        for low in range(2)
                    ]
                    strips.append(jnp.concatenate(pair, axis=1))
            stacked = jnp.concatenate(strips, axis=0)
            chosen = jnp.where(row_ids == target, 1.0, 0.0)
            picked = jnp.dot(
                stacked, chosen.astype(jnp.bfloat16), preferred_element_type=jnp.float32
            )
            send_buf[atom] = picked.astype(jnp.bfloat16).reshape(2 * pieces, energy_dev, ORB)

        def atom_step(index, inner):
            for j in range(unroll):
                pick_atom(index * unroll + j)
            return inner

        lax.fori_loop(0, ATL // unroll, atom_step, 0)

    def layer_step(step, carry):
        layer_pairs(layer_at(step))
        for phase in range(early):
            start_sends(phase, layer_at(step))
        return carry

    def mask_coupling():
        shape = (NORB, PAIR)
        column = lax.broadcasted_iota(jnp.int32, shape, 0)
        entry = lax.broadcasted_iota(jnp.int32, shape, 1)
        outer, inner = lax.div(entry, NORB), lax.rem(entry, NORB)
        for slot in range(NBR):
            coupling_copy(slot).wait()
        for atom in range(atom_dev):
            place = me * atom_dev + atom
            own = orbitals_ref[place]
            kept = (outer < own) & (inner < own)
            masks = [
                jnp.where(kept & (column < orbitals_ref[neighbours_ref[near, place]]), 1.0, 0.0)
                for near in range(NBR)
            ]

            def row_step(row, carry):
                used = jnp.where(row < own, 1.0, 0.0)
                for near in range(NBR):
                    block = coupling_buf[atom, row, near].astype(jnp.float32)
                    coupling_buf[atom, row, near] = (block * (masks[near] * used)).astype(
                        jnp.bfloat16
                    )
                return carry

            lax.fori_loop(0, NORB, row_step, 0)

    def spread_phonon():
        for other in range(mom_count):
            mode = modes_ref[mom, other]
            rows = phonon_ref[mode]
            for part in range(2):
                wide = jnp.broadcast_to(rows[part : part + 1], (ORB, rows.shape[1]))
                kernel_buf[other, part] = wide.T

    def start_sends(phase, layer):
        for offset in range(dev_layer):
            dest = layer * dev_layer + offset

            @pl.when(dest != me)
            def _():
                if phase >= early:
                    send_copy(phase - early, dest).wait_send()
                send_copy(phase, dest).start()

            @pl.when(dest == me)
            def _():
                own_copy(phase).start()

    def finish(phase):
        start, size = phases[phase]
        for step in range(1, mom_count):
            mom_copy(phase, step, False).wait_recv()
        for atom in range(start, start + size):
            sums = [0.0, 0.0]
            for other in range(mom_count):
                wide_re = jnp.concatenate([kernel_buf[other, 0]] * (PAIR // ORB), axis=1)
                wide_im = jnp.concatenate([kernel_buf[other, 1]] * (PAIR // ORB), axis=1)
                time_re = time_buf[other, atom, 0].astype(jnp.float32)
                time_im = time_buf[other, atom, 1].astype(jnp.float32)
                sums[0] = sums[0] + (wide_re * time_re - wide_im * time_im)
                sums[1] = sums[1] + (wide_re * time_im + wide_im * time_re)
            conv_re = sums[0].astype(jnp.bfloat16)
            conv_im = sums[1].astype(jnp.bfloat16)
            dot = functools.partial(jnp.dot, preferred_element_type=jnp.float32)
            scale = 1.0 / cos_ref.shape[0]
            res_re = (dot(cos_ref[...], conv_re) - dot(sin_ref[...], conv_im)) * scale
            res_im = (dot(cos_ref[...], conv_im) + dot(sin_ref[...], conv_re)) * scale
            base = atom * 2 * PAIR
            out_ref[:, base : base + PAIR] = res_re.astype(jnp.bfloat16)
            out_ref[:, base + PAIR : base + 2 * PAIR] = res_im.astype(jnp.bfloat16)

    def transform(phase):
        start, size = phases[phase]

        def arrive(source, carry):
            @pl.when(source != me)
            def _():
                arrive_copy(phase, source).wait_recv()

            return carry

        lax.fori_loop(0, shard_count, arrive, 0)
        own_copy(phase).wait()
        energies = shard_count * energy_dev
        for atom in range(start, start + size):
            coupled = []
            for part in range(2):
                total = 0.0
                for piece in range(0, pieces, 2):
                    block = jnp.concatenate(
                        [
                            recv_buf[atom, :, part * pieces + piece + low].reshape(energies, ORB)
                            for low in range(2)
                        ],
                        axis=1,
                    )
                    total = total + jnp.dot(
                        block,
                        coupling_buf[atom, 2 * piece : 2 * piece + 4].reshape(PAIR, PAIR),
                        preferred_element_type=jnp.float32,
                    )
                coupled.append(total.astype(jnp.bfloat16))
            dot = functools.partial(jnp.dot, preferred_element_type=jnp.float32)
            time_re = dot(cos_ref[...], coupled[0]) + dot(sin_ref[...], coupled[1])
            time_im = dot(cos_ref[...], coupled[1]) - dot(sin_ref[...], coupled[0])
            time_buf[mom, atom, 0] = time_re.astype(jnp.bfloat16)
            time_buf[mom, atom, 1] = time_im.astype(jnp.bfloat16)
        for step in range(1, mom_count):
            mom_copy(phase, step, True).start()

    layer_pairs(layer_at(0))
    pl.semaphore_wait(barrier, shard_count + mom_count - 2)
    for phase in range(early):
        start_sends(phase, layer_at(0))
    lax.fori_loop(1, layers, layer_step, 0)
    for copy in small[4:]:
        copy.wait()
    mask_coupling()
    spread_phonon()

    def send_phase(phase):
        def more(step, carry):
            start_sends(phase, layer_at(step))
            return carry

        lax.fori_loop(0, layers, more, 0)

    done = 0
    for phase in range(len(phases)):
        if phase + 2 <= last and phase + 2 >= early:
            send_phase(phase + 2)
        transform(phase)
        if phase >= 2 or phase == last:
            while done < phase:
                finish(done)
                done += 1
        elif phase == 1:
            finish(0)
            done = 1
    finish(last)

    def drain(dest, carry):
        @pl.when(dest != me)
        def _():
            for phase in range(max(len(phases) - early, 0), len(phases)):
                send_copy(phase, dest).wait_send()

        return carry

    lax.fori_loop(0, shard_count, drain, 0)
    for phase in range(len(phases)):
        for step in range(1, mom_count):
            mom_copy(phase, step, True).wait_send()


def fused(shard_count, mom_count, green_ret, broadening, occupation, neighbours, orbitals,
          coupling, phonon, mode_table):
    greens = green_ret[0]
    energy_dev = greens.shape[0]
    atom_dev = coupling.shape[0]
    energies = phonon.shape[-1]
    counter = np.arange(energies, dtype=np.int32)
    angles = (counter[:, None] * counter[None, :] % energies).astype(np.float32)
    angles = angles * np.float32(2.0 * math.pi / energies)
    cos_table = jnp.asarray(np.cos(angles), jnp.bfloat16)
    sin_table = jnp.asarray(np.sin(angles), jnp.bfloat16)
    blocks = coupling.reshape(atom_dev, NBR, NORB, NORB, PAIR)
    phases = phase_plan(atom_dev)
    count = len(phases)
    vmem = pl.BlockSpec(memory_space=pltpu.VMEM)
    hbm = pl.BlockSpec(memory_space=pl.ANY)
    smem = pltpu.SMEM
    dma = pltpu.SemaphoreType.DMA
    result = pl.pallas_call(
        functools.partial(fused_kernel, phases, shard_count, mom_count),
        out_shape=jax.ShapeDtypeStruct((energies, atom_dev * 2 * PAIR), jnp.bfloat16),
        in_specs=[hbm] * 10,
        out_specs=vmem,
        scratch_shapes=[
            pltpu.VMEM(broadening.shape, broadening.dtype),
            smem(occupation.shape, occupation.dtype),
            smem(neighbours.shape[::-1], neighbours.dtype),
            smem(orbitals.shape, orbitals.dtype),
            pltpu.VMEM(phonon.shape, phonon.dtype),
            smem(mode_table.shape, mode_table.dtype),
            pltpu.VMEM(cos_table.shape, cos_table.dtype),
            pltpu.VMEM(sin_table.shape, sin_table.dtype),
            dma((8,)),
            pltpu.VMEM((LAYERS, energy_dev, 2, ORB, ORB), jnp.bfloat16),
            pltpu.VMEM((2, energy_dev * ORB, ORB), jnp.float32),
            pltpu.VMEM((ATOMS, NORB, energy_dev, ORB), jnp.bfloat16),
            pltpu.VMEM((atom_dev, shard_count, NORB, energy_dev, ORB), jnp.bfloat16),
            pltpu.VMEM((atom_dev, NORB, NBR, NORB, PAIR), jnp.bfloat16),
            pltpu.VMEM((mom_count, 2, energies, ORB), jnp.float32),
            pltpu.VMEM((2 * ORB, 2 * ORB), jnp.bfloat16),
            pltpu.VMEM((mom_count, atom_dev, 2, energies, PAIR), jnp.bfloat16),
            dma((LAYERS,)),
            dma((NBR,)),
            dma((count,)),
            dma((count, shard_count)),
            dma((count, shard_count)),
            dma((count, max(mom_count - 1, 1))),
            dma((count, max(mom_count - 1, 1))),
        ],
        compiler_params=pltpu.CompilerParams(
            collective_id=0, has_side_effects=True, vmem_limit_bytes=56 * 1024 * 1024
        ),
    )(
        greens, broadening, occupation, neighbours.T, orbitals, blocks, phonon, mode_table,
        cos_table, sin_table,
    )
    return result.reshape(1, energies, atom_dev, 2, PAIR)


def solution(mesh):
    in_specs = (
        P("mom", "shard", None, None, None, None),
        P(),
        P("mom", "shard"),
        P(),
        P(),
        P("shard", None, None, None),
        P(),
        P(),
    )
    out_specs = P("mom", None, "shard", None, None)
    shard_count, mom_count = mesh.shape["shard"], mesh.shape["mom"]

    def body(*args):
        energy_dev, atom_dev = args[0].shape[1], args[5].shape[0]
        if energy_dev % 16 == 0 and ATL % atom_dev == 0:
            return fused(shard_count, mom_count, *args)
        return local(*args)

    return jax.shard_map(body, mesh=mesh, in_specs=in_specs, out_specs=out_specs, check_vma=False)
```

```python
import functools
import math

import jax
import jax.numpy as jnp
import numpy as np
from jax import lax
from jax.experimental import pallas as pl
from jax.experimental.pallas import tpu as pltpu
from jax.sharding import PartitionSpec as P

NORB = 16
ATL = 8
NBR = 4
ENERGIES = 256
LAYERS = 8
ORB = 128
PAIR = 256
ATOMS = 64


def dft_tables(length):
    counter = jnp.arange(length, dtype=jnp.int32)
    phases = counter[:, None] * counter[None, :] % length
    angles = phases.astype(jnp.float32) * (2.0 * math.pi / length)
    return (jnp.cos(angles).astype(jnp.bfloat16), jnp.sin(angles).astype(jnp.bfloat16))


def local(green_ret, broadening, occupation, neighbours, orbitals, coupling, phonon, mode_table):
    highest = lax.Precision.HIGHEST
    greens = green_ret[0]
    energy_dev = greens.shape[0]
    mixing = jnp.stack(
        [
            jnp.concatenate([broadening[0], broadening[1]], axis=1),
            jnp.concatenate([-broadening[1], broadening[0]], axis=1),
        ],
        axis=0,
    )
    left = jnp.einsum("elpik,pkq->eliq", greens, mixing, preferred_element_type=jnp.float32).astype(
        jnp.bfloat16
    )
    slot_atoms = neighbours % ATL
    selector = slot_atoms[:, :, None] == jnp.arange(ATL, dtype=jnp.int32)[None, None, :]
    layer_orbitals = jnp.repeat(orbitals.reshape(LAYERS, ATL), ATL, axis=0)
    partner_count = jnp.sum(jnp.where(selector, layer_orbitals[:, None, :], 0), axis=2)
    green_rows = greens.reshape(energy_dev, LAYERS, 2, ATL, NORB, ORB)
    select_bf = selector.reshape(LAYERS, ATL, NBR, ATL).astype(jnp.bfloat16)
    partner_rows = jnp.einsum(
        "ljnm,elpmic->eljnpic", select_bf, green_rows, preferred_element_type=jnp.float32
    ).astype(jnp.bfloat16)
    partner_re = partner_rows[:, :, :, :, 0]
    partner_im = partner_rows[:, :, :, :, 1]
    left_rows_re = left[..., :ORB].reshape(energy_dev, LAYERS, ATL, NORB, ORB)
    left_rows_im = left[..., ORB:].reshape(energy_dev, LAYERS, ATL, NORB, ORB)
    pair_re = jnp.einsum(
        "eljic,eljnkc->eljnik", left_rows_re, partner_re, preferred_element_type=jnp.float32
    ) + jnp.einsum(
        "eljic,eljnkc->eljnik", left_rows_im, partner_im, preferred_element_type=jnp.float32
    )
    pair_im = jnp.einsum(
        "eljic,eljnkc->eljnik", left_rows_im, partner_re, preferred_element_type=jnp.float32
    ) - jnp.einsum(
        "eljic,eljnkc->eljnik", left_rows_re, partner_im, preferred_element_type=jnp.float32
    )
    chosen = jnp.stack([pair_re, pair_im], axis=4)
    chosen = chosen.reshape(energy_dev, ATOMS, NBR, 2, NORB, NORB)
    counter = jnp.arange(NORB, dtype=jnp.int32)
    row_mask = counter[None, :] < orbitals[:, None]
    column_mask = counter[None, None, :] < partner_count[:, :, None]
    pair_mask = (row_mask[:, None, :, None] & column_mask[:, :, None, :]).astype(jnp.float32)
    scaled = (
        chosen * occupation[0][:, None, None, None, None, None] * pair_mask[None, :, :, None, :, :]
    )
    pair_blocks = scaled.reshape(energy_dev, ATOMS, NBR, 2, PAIR).astype(jnp.bfloat16)
    arrived = lax.all_to_all(pair_blocks, "shard", split_axis=1, concat_axis=0, tiled=True)
    atom_dev = arrived.shape[1]
    mixed_terms = jnp.einsum(
        "eanpx,anxy->eapy", arrived, coupling, preferred_element_type=jnp.float32
    )
    first_atom = lax.axis_index("shard") * atom_dev
    own_orbitals = lax.dynamic_slice_in_dim(orbitals, first_atom, atom_dev)
    pair_index = jnp.arange(PAIR, dtype=jnp.int32)
    own_mask = (
        (pair_index[None, :] // NORB < own_orbitals[:, None])
        & (pair_index[None, :] % NORB < own_orbitals[:, None])
    ).astype(jnp.float32)
    coupled = (mixed_terms * own_mask[None, :, None, :]).astype(jnp.bfloat16)
    cos_table, sin_table = dft_tables(ENERGIES)
    flat_coupled = coupled.reshape(ENERGIES, -1)
    part_cos = jnp.dot(cos_table, flat_coupled, preferred_element_type=jnp.float32).reshape(
        ENERGIES, atom_dev, 2, PAIR
    )
    part_sin = jnp.dot(sin_table, flat_coupled, preferred_element_type=jnp.float32).reshape(
        ENERGIES, atom_dev, 2, PAIR
    )
    time_data = jnp.stack(
        [part_cos[:, :, 0] + part_sin[:, :, 1], part_cos[:, :, 1] - part_sin[:, :, 0]], axis=2
    ).astype(jnp.bfloat16)
    own_momentum = lax.axis_index("mom")
    mode_count = phonon.shape[0]
    mode_ids = jnp.arange(mode_count, dtype=jnp.int32)
    own_modes = lax.dynamic_slice_in_dim(mode_table, own_momentum, 1, 0)[0]
    phonon_flat = phonon.reshape(mode_count, -1)
    received = lax.all_gather(time_data[None], "mom", axis=0, tiled=True)
    row_count = received.shape[0]
    one_hot = (own_modes[:, None] == mode_ids[None, :]).astype(jnp.float32)
    kernel = jnp.dot(one_hot, phonon_flat, precision=highest).reshape(row_count, 2, ENERGIES)
    values = received.astype(jnp.float32)
    kernel_re = kernel[:, 0][:, :, None, None]
    kernel_im = kernel[:, 1][:, :, None, None]
    add_re = jnp.sum(kernel_re * values[:, :, :, 0] - kernel_im * values[:, :, :, 1], axis=0)
    add_im = jnp.sum(kernel_re * values[:, :, :, 1] + kernel_im * values[:, :, :, 0], axis=0)
    summed = jnp.stack([add_re, add_im], axis=2)
    convolved = summed.astype(jnp.bfloat16)
    flat_conv = convolved.reshape(ENERGIES, -1)
    back_cos = jnp.dot(cos_table, flat_conv, preferred_element_type=jnp.float32).reshape(
        ENERGIES, atom_dev, 2, PAIR
    )
    back_sin = jnp.dot(sin_table, flat_conv, preferred_element_type=jnp.float32).reshape(
        ENERGIES, atom_dev, 2, PAIR
    )
    result_re = (back_cos[:, :, 0] - back_sin[:, :, 1]) * (1.0 / ENERGIES)
    result_im = (back_cos[:, :, 1] + back_sin[:, :, 0]) * (1.0 / ENERGIES)
    return jnp.stack([result_re, result_im], axis=2)[None].astype(jnp.bfloat16)


MESH = pl.DeviceIdType.MESH


def phase_plan(atom_dev, shared):
    return [(0, shared)] + [(start, 1) for start in range(shared, atom_dev)]


def fused_kernel(
    phases,
    shard_count,
    mom_count,
    green_hbm,
    broadening_hbm,
    occupation_hbm,
    neighbours_hbm,
    orbitals_hbm,
    coupling_hbm,
    phonon_hbm,
    modes_hbm,
    cos_hbm,
    sin_hbm,
    out_ref,
    broadening_ref,
    occupation_ref,
    neighbours_ref,
    orbitals_ref,
    phonon_ref,
    modes_ref,
    cos_ref,
    sin_ref,
    small_sem,
    green_buf,
    full_buf,
    send_buf,
    recv_buf,
    coupling_buf,
    kernel_buf,
    mixing_ref,
    mirror_buf,
    coupled_buf,
    part_buf,
    time_buf,
    green_sem,
    coupling_sem,
    own_sem,
    send_sem,
    recv_sem,
    mom_send_sem,
    mom_recv_sem,
    mirror_sem,
    forward_send_sem,
    forward_recv_sem,
    part_sem,
):
    me = lax.axis_index("shard")
    mom = lax.axis_index("mom")
    layers, energy_dev = green_buf.shape[0], green_buf.shape[1]
    atom_dev = recv_buf.shape[0]
    dev_layer = ATL // atom_dev
    half = layers // 2
    pieces = NORB // 2
    last = len(phases) - 1
    early = min(2, len(phases))
    shared = phases[0][1]
    half_count = shard_count // 2
    my_half = lax.div(me, half_count)
    my_rank = lax.rem(me, half_count)
    mirror = lax.rem(me + half_count, shard_count)
    half_rows = half_count * energy_dev

    def layer_at(step):
        home = lax.div(me, dev_layer)
        side = lax.rem(lax.div(home, half) + 1 + step, 2)
        return side * half + lax.rem(home + lax.div(step, 2), half)

    def green_copy(layer):
        return pltpu.make_async_copy(
            green_hbm.at[:, layer], green_buf.at[layer], green_sem.at[layer]
        )

    def coupling_copy():
        return pltpu.make_async_copy(coupling_hbm, coupling_buf, coupling_sem)

    def mirror_copy():
        return pltpu.make_async_remote_copy(
            src_ref=coupling_hbm.at[mom],
            dst_ref=mirror_buf.at[mom],
            send_sem=mirror_sem.at[0],
            recv_sem=mirror_sem.at[1],
            device_id={"shard": mirror},
            device_id_type=MESH,
        )

    def forward_copy(step, sending):
        source = lax.rem(mom + mom_count - step, mom_count)
        return pltpu.make_async_remote_copy(
            src_ref=mirror_buf.at[mom],
            dst_ref=mirror_buf.at[mom if sending else source],
            send_sem=forward_send_sem.at[step - 1],
            recv_sem=forward_recv_sem.at[step - 1],
            device_id={"mom": lax.rem(mom + step, mom_count)},
            device_id_type=MESH,
        )

    def part_copy(sending):
        origin = my_half if sending else 1 - my_half
        rows = pl.ds(pl.multiple_of(origin * half_rows, half_rows), half_rows)
        return pltpu.make_async_remote_copy(
            src_ref=part_buf,
            dst_ref=coupled_buf.at[:, :, rows],
            send_sem=part_sem.at[0],
            recv_sem=part_sem.at[1],
            device_id={"shard": mirror},
            device_id_type=MESH,
        )

    def route(phase, dest):
        if phase > 0:
            return dest, me
        crossing = lax.rem(my_half + lax.div(dest, half_count), 2)
        target = my_half * half_count + lax.rem(dest, half_count)
        return target, crossing * half_count + my_rank

    def own_copy(phase, dest):
        start, size = phases[phase]
        slot = route(phase, dest)[1]
        crossing = lax.rem(my_half + lax.div(dest, half_count), 2) if phase == 0 else 0
        return pltpu.make_async_copy(
            send_buf.at[pl.ds(dest * atom_dev + start, size)],
            recv_buf.at[pl.ds(start, size), slot],
            own_sem.at[phase + crossing * len(phases)],
        )

    def send_copy(phase, dest):
        start, size = phases[phase]
        target, slot = route(phase, dest)
        return pltpu.make_async_remote_copy(
            src_ref=send_buf.at[pl.ds(dest * atom_dev + start, size)],
            dst_ref=recv_buf.at[pl.ds(start, size), slot],
            send_sem=send_sem.at[phase, dest],
            recv_sem=recv_sem.at[phase, slot],
            device_id={"shard": target},
            device_id_type=MESH,
        )

    def arrive_copy(phase, slot, source):
        start, size = phases[phase]
        return pltpu.make_async_remote_copy(
            src_ref=send_buf.at[pl.ds(source * atom_dev + start, size)],
            dst_ref=recv_buf.at[pl.ds(start, size), slot],
            send_sem=send_sem.at[phase, source],
            recv_sem=recv_sem.at[phase, slot],
            device_id={"shard": source},
            device_id_type=MESH,
        )

    def mom_copy(phase, step, sending):
        start, size = phases[phase]
        dest = lax.rem(mom + step, mom_count)
        source = lax.rem(mom + mom_count - step, mom_count)
        origin = mom if sending else source
        return pltpu.make_async_remote_copy(
            src_ref=time_buf.at[mom, pl.ds(start, size)],
            dst_ref=time_buf.at[origin, pl.ds(start, size)],
            send_sem=mom_send_sem.at[phase, step - 1],
            recv_sem=mom_recv_sem.at[phase, step - 1],
            device_id={"mom": dest},
            device_id_type=MESH,
        )

    small = [
        (broadening_hbm, broadening_ref),
        (occupation_hbm, occupation_ref),
        (neighbours_hbm, neighbours_ref),
        (orbitals_hbm, orbitals_ref),
        (phonon_hbm, phonon_ref),
        (modes_hbm, modes_ref),
        (cos_hbm, cos_ref),
        (sin_hbm, sin_ref),
    ]
    small = [
        pltpu.make_async_copy(source, held, small_sem.at[index])
        for index, (source, held) in enumerate(small)
    ]
    for copy in small[:4]:
        copy.start()
    for step in range(layers):
        green_copy(layer_at(step)).start()
    for copy in small[4:]:
        copy.start()
    coupling_copy().start()

    barrier = pltpu.get_barrier_semaphore()
    for step in range(1, shard_count):
        pl.semaphore_signal(
            barrier,
            inc=1,
            device_id={"shard": lax.rem(me + step, shard_count)},
            device_id_type=MESH,
        )
    for step in range(1, mom_count):
        pl.semaphore_signal(
            barrier,
            inc=1,
            device_id={"mom": lax.rem(mom + step, mom_count)},
            device_id_type=MESH,
        )
    for copy in small[:4]:
        copy.wait()
    mixing_ref[:ORB, :ORB] = broadening_ref[0]
    mixing_ref[:ORB, ORB:] = broadening_ref[1]
    mixing_ref[ORB:, :ORB] = -broadening_ref[1]
    mixing_ref[ORB:, ORB:] = broadening_ref[0]
    pl.semaphore_wait(barrier, shard_count + mom_count - 2)
    mirror_copy().start()
    group = 8
    unroll = 4

    def layer_pairs(layer):
        green_copy(layer).wait()

        def energy_step(index, inner):
            first = index * group
            joined = [
                jnp.concatenate(
                    [green_buf[layer, first + j, 0], green_buf[layer, first + j, 1]], axis=1
                )
                for j in range(group)
            ]
            left = jnp.dot(
                jnp.concatenate(joined, axis=0),
                mixing_ref[...],
                preferred_element_type=jnp.float32,
            ).astype(jnp.bfloat16)
            for j in range(group):
                turned = jnp.concatenate(
                    [-joined[j][:, ORB:], joined[j][:, :ORB]], axis=1
                )
                full = lax.dot_general(
                    left[j * ORB : (j + 1) * ORB],
                    jnp.concatenate([joined[j], turned], axis=0),
                    (((1,), (1,)), ((), ())),
                    preferred_element_type=jnp.float32,
                )
                full = full * occupation_ref[0, first + j]
                rows = pl.ds(pl.multiple_of((first + j) * ORB, ORB), ORB)
                full_buf[0, rows, :] = full[:, :ORB]
                full_buf[1, rows, :] = full[:, ORB:]
            return inner

        lax.fori_loop(0, energy_dev // group, energy_step, 0)

        lane = lax.broadcasted_iota(jnp.int32, (1, ORB), 1)
        lane_slot = lax.rem(lax.div(lane, NORB), NBR)
        lane_base = lax.rem(lane, NORB) + lax.div(lane, NORB * NBR) * ORB
        row_ids = lax.broadcasted_iota(jnp.int32, (2 * ORB, ORB), 0)

        def pick_atom(slot):
            atom = layer * ATL + slot
            target = lane_base
            for near in range(NBR):
                start = (neighbours_ref[near, atom] - layer * ATL) * NORB
                target = target + jnp.where(lane_slot == near, start, 0)
            strips = []
            for part in range(2):
                for piece in range(pieces):
                    pair = [
                        full_buf[
                            part,
                            pl.ds(slot * NORB + 2 * piece + low, energy_dev, stride=ORB),
                            :,
                        ].astype(jnp.bfloat16)
                        for low in range(2)
                    ]
                    strips.append(jnp.concatenate(pair, axis=1))
            stacked = jnp.concatenate(strips, axis=0)
            chosen = jnp.where(row_ids == target, 1.0, 0.0)
            picked = jnp.dot(
                stacked, chosen.astype(jnp.bfloat16), preferred_element_type=jnp.float32
            )
            send_buf[atom] = picked.astype(jnp.bfloat16).reshape(2 * pieces, energy_dev, ORB)

        def atom_step(index, inner):
            for j in range(unroll):
                pick_atom(index * unroll + j)
            return inner

        lax.fori_loop(0, ATL // unroll, atom_step, 0)

    def layer_step(step, carry):
        layer_pairs(layer_at(step))
        for phase in range(early):
            start_sends(phase, layer_at(step))

        @pl.when(step == layers - 2)
        def _():
            mirror_copy().wait_recv()
            for other in range(1, mom_count):
                forward_copy(other, True).start()

        return carry

    def mask_coupling(buffer, atom, place):
        shape = (NORB, PAIR)
        column = lax.broadcasted_iota(jnp.int32, shape, 0)
        entry = lax.broadcasted_iota(jnp.int32, shape, 1)
        outer, inner = lax.div(entry, NORB), lax.rem(entry, NORB)
        own = orbitals_ref[place]
        kept = (outer < own) & (inner < own)
        masks = [
            jnp.where(kept & (column < orbitals_ref[neighbours_ref[near, place]]), 1.0, 0.0)
            for near in range(NBR)
        ]

        def row_step(row, carry):
            used = jnp.where(row < own, 1.0, 0.0)
            for near in range(NBR):
                block = buffer[atom, near, row].astype(jnp.float32)
                buffer[atom, near, row] = (block * (masks[near] * used)).astype(jnp.bfloat16)
            return carry

        lax.fori_loop(0, NORB, row_step, 0)

    def spread_phonon():
        for other in range(mom_count):
            mode = modes_ref[mom, other]
            rows = phonon_ref[mode]
            for part in range(2):
                wide = jnp.broadcast_to(rows[part : part + 1], (ORB, rows.shape[1]))
                kernel_buf[other, part] = wide.T

    def start_sends(phase, layer):
        for offset in range(dev_layer):
            dest = layer * dev_layer + offset
            if phase >= early:
                before = phase - early

                @pl.when(route(before, dest)[0] != me)
                def _():
                    send_copy(before, dest).wait_send()

            target = route(phase, dest)[0]

            @pl.when(target != me)
            def _():
                send_copy(phase, dest).start()

            @pl.when(target == me)
            def _():
                own_copy(phase, dest).start()

    def finish(phase):
        start, size = phases[phase]
        for step in range(1, mom_count):
            mom_copy(phase, step, False).wait_recv()
        for atom in range(start, start + size):
            sums = [0.0, 0.0]
            for other in range(mom_count):
                wide_re = jnp.concatenate([kernel_buf[other, 0]] * (PAIR // ORB), axis=1)
                wide_im = jnp.concatenate([kernel_buf[other, 1]] * (PAIR // ORB), axis=1)
                time_re = time_buf[other, atom, 0].astype(jnp.float32)
                time_im = time_buf[other, atom, 1].astype(jnp.float32)
                sums[0] = sums[0] + (wide_re * time_re - wide_im * time_im)
                sums[1] = sums[1] + (wide_re * time_im + wide_im * time_re)
            conv_re = sums[0].astype(jnp.bfloat16)
            conv_im = sums[1].astype(jnp.bfloat16)
            scale = 1.0 / cos_ref.shape[0]
            res_re = (dot(cos_ref[...], conv_re) - dot(sin_ref[...], conv_im)) * scale
            res_im = (dot(cos_ref[...], conv_im) + dot(sin_ref[...], conv_re)) * scale
            base = atom * 2 * PAIR
            out_ref[:, base : base + PAIR] = res_re.astype(jnp.bfloat16)
            out_ref[:, base + PAIR : base + 2 * PAIR] = res_im.astype(jnp.bfloat16)

    dot = functools.partial(jnp.dot, preferred_element_type=jnp.float32)

    def arrive_all(phase):
        def arrive(slot, carry):
            source = slot
            if phase == 0:
                source = my_half * half_count + lax.rem(slot, half_count)

            @pl.when(source != me)
            def _():
                arrive_copy(phase, slot, source).wait_recv()

            return carry

        lax.fori_loop(0, shard_count, arrive, 0)
        own_copy(phase, me).wait()
        if phase == 0:
            own_copy(phase, mirror).wait()

    def couple(atom, weights, place, first, count):
        result = []
        for part in range(2):
            total = 0.0
            for piece in range(0, pieces, 2):
                block = jnp.concatenate(
                    [
                        recv_buf[
                            atom, first : first + count, part * pieces + piece + low
                        ].reshape(count * energy_dev, ORB)
                        for low in range(2)
                    ],
                    axis=1,
                )
                matrix = jnp.concatenate(
                    [
                        weights[place, near, row]
                        for row in range(2 * piece, 2 * piece + 4)
                        for near in range(NBR)
                    ],
                    axis=0,
                )
                total = total + dot(block, matrix)
            result.append(total.astype(jnp.bfloat16))
        return result

    def to_time(atom, coupled):
        time_re = dot(cos_ref[...], coupled[0]) + dot(sin_ref[...], coupled[1])
        time_im = dot(cos_ref[...], coupled[1]) - dot(sin_ref[...], coupled[0])
        time_buf[mom, atom, 0] = time_re.astype(jnp.bfloat16)
        time_buf[mom, atom, 1] = time_im.astype(jnp.bfloat16)

    def mirror_part():
        for other in range(1, mom_count):
            forward_copy(other, True).wait_send()
            forward_copy(other, False).wait_recv()
        for atom in range(shared):
            mask_coupling(mirror_buf, atom, mirror * atom_dev + atom)
        arrive_all(0)
        for atom in range(shared):
            far = couple(atom, mirror_buf, atom, half_count, half_count)
            for part in range(2):
                part_buf[atom, part] = far[part]
        part_copy(True).start()
        rows = pl.ds(pl.multiple_of(my_half * half_rows, half_rows), half_rows)
        for atom in range(shared):
            near = couple(atom, coupling_buf, atom, 0, half_count)
            for part in range(2):
                coupled_buf[atom, part, rows, :] = near[part]

    def transform(phase):
        start, size = phases[phase]
        if phase == 0:
            mirror_part()
            part_copy(False).wait_recv()
            for atom in range(size):
                to_time(atom, [coupled_buf[atom, 0], coupled_buf[atom, 1]])
        else:
            arrive_all(phase)
            for atom in range(start, start + size):
                to_time(atom, couple(atom, coupling_buf, atom, 0, shard_count))
        for step in range(1, mom_count):
            mom_copy(phase, step, True).start()

    lax.fori_loop(0, layers, layer_step, 0)
    for copy in small[4:]:
        copy.wait()
    coupling_copy().wait()
    for atom in range(atom_dev):
        mask_coupling(coupling_buf, atom, me * atom_dev + atom)
    spread_phonon()

    def send_phase(phase):
        def more(step, carry):
            start_sends(phase, layer_at(step))
            return carry

        lax.fori_loop(0, layers, more, 0)

    done = 0
    for phase in range(len(phases)):
        if phase + 2 <= last and phase + 2 >= early:
            send_phase(phase + 2)
        transform(phase)
        if phase >= 2 or phase == last:
            while done < phase:
                finish(done)
                done += 1
        elif phase == 1:
            finish(0)
            done = 1
    finish(last)

    def drain(dest, carry):
        for phase in range(max(len(phases) - early, 0), len(phases)):

            @pl.when(route(phase, dest)[0] != me)
            def _():
                send_copy(phase, dest).wait_send()

        return carry

    lax.fori_loop(0, shard_count, drain, 0)
    mirror_copy().wait_send()
    part_copy(True).wait_send()
    for phase in range(len(phases)):
        for step in range(1, mom_count):
            mom_copy(phase, step, True).wait_send()


def fused(shard_count, mom_count, green_ret, broadening, occupation, neighbours, orbitals,
          coupling, phonon, mode_table):
    greens = green_ret[0]
    energy_dev = greens.shape[0]
    atom_dev = coupling.shape[0]
    energies = phonon.shape[-1]
    counter = np.arange(energies, dtype=np.int32)
    angles = (counter[:, None] * counter[None, :] % energies).astype(np.float32)
    angles = angles * np.float32(2.0 * math.pi / energies)
    cos_table = jnp.asarray(np.cos(angles), jnp.bfloat16)
    sin_table = jnp.asarray(np.sin(angles), jnp.bfloat16)
    blocks = coupling.reshape(atom_dev, NBR, NORB, NORB, PAIR)
    shared = mom_count
    phases = phase_plan(atom_dev, shared)
    count = len(phases)
    vmem = pl.BlockSpec(memory_space=pltpu.VMEM)
    hbm = pl.BlockSpec(memory_space=pl.ANY)
    smem = pltpu.SMEM
    dma = pltpu.SemaphoreType.DMA
    result = pl.pallas_call(
        functools.partial(fused_kernel, phases, shard_count, mom_count),
        out_shape=jax.ShapeDtypeStruct((energies, atom_dev * 2 * PAIR), jnp.bfloat16),
        in_specs=[hbm] * 10,
        out_specs=vmem,
        scratch_shapes=[
            pltpu.VMEM(broadening.shape, broadening.dtype),
            smem(occupation.shape, occupation.dtype),
            smem(neighbours.shape[::-1], neighbours.dtype),
            smem(orbitals.shape, orbitals.dtype),
            pltpu.VMEM(phonon.shape, phonon.dtype),
            smem(mode_table.shape, mode_table.dtype),
            pltpu.VMEM(cos_table.shape, cos_table.dtype),
            pltpu.VMEM(sin_table.shape, sin_table.dtype),
            dma((8,)),
            pltpu.VMEM((LAYERS, energy_dev, 2, ORB, ORB), jnp.bfloat16),
            pltpu.VMEM((2, energy_dev * ORB, ORB), jnp.float32),
            pltpu.VMEM((ATOMS, NORB, energy_dev, ORB), jnp.bfloat16),
            pltpu.VMEM((atom_dev, shard_count, NORB, energy_dev, ORB), jnp.bfloat16),
            pltpu.VMEM((atom_dev, NBR, NORB, NORB, PAIR), jnp.bfloat16),
            pltpu.VMEM((mom_count, 2, energies, ORB), jnp.float32),
            pltpu.VMEM((2 * ORB, 2 * ORB), jnp.bfloat16),
            pltpu.VMEM((shared, NBR, NORB, NORB, PAIR), jnp.bfloat16),
            pltpu.VMEM((shared, 2, energies, PAIR), jnp.bfloat16),
            pltpu.VMEM((shared, 2, energies // 2, PAIR), jnp.bfloat16),
            pltpu.VMEM((mom_count, atom_dev, 2, energies, PAIR), jnp.bfloat16),
            dma((LAYERS,)),
            dma,
            dma((2 * count,)),
            dma((count, shard_count)),
            dma((count, shard_count)),
            dma((count, max(mom_count - 1, 1))),
            dma((count, max(mom_count - 1, 1))),
            dma((2,)),
            dma((max(mom_count - 1, 1),)),
            dma((max(mom_count - 1, 1),)),
            dma((2,)),
        ],
        compiler_params=pltpu.CompilerParams(
            collective_id=0, has_side_effects=True, vmem_limit_bytes=56 * 1024 * 1024
        ),
    )(
        greens, broadening, occupation, neighbours.T, orbitals, blocks, phonon, mode_table,
        cos_table, sin_table,
    )
    return result.reshape(1, energies, atom_dev, 2, PAIR)


def solution(mesh):
    in_specs = (
        P("mom", "shard", None, None, None, None),
        P(),
        P("mom", "shard"),
        P(),
        P(),
        P("shard", None, None, None),
        P(),
        P(),
    )
    out_specs = P("mom", None, "shard", None, None)
    shard_count, mom_count = mesh.shape["shard"], mesh.shape["mom"]

    def body(*args):
        energy_dev, atom_dev = args[0].shape[1], args[5].shape[0]
        if energy_dev % 16 == 0 and ATL % atom_dev == 0 and atom_dev >= mom_count + 2:
            return fused(shard_count, mom_count, *args)
        return local(*args)

    return jax.shard_map(body, mesh=mesh, in_specs=in_specs, out_specs=out_specs, check_vma=False)
```

```python
import functools
import math

import jax
import jax.numpy as jnp
import numpy as np
from jax import lax
from jax.experimental import pallas as pl
from jax.experimental.pallas import tpu as pltpu
from jax.sharding import PartitionSpec as P

NORB = 16
ATL = 8
NBR = 4
ENERGIES = 256
LAYERS = 8
ORB = 128
PAIR = 256
ATOMS = 64


def dft_tables(length):
    counter = jnp.arange(length, dtype=jnp.int32)
    phases = counter[:, None] * counter[None, :] % length
    angles = phases.astype(jnp.float32) * (2.0 * math.pi / length)
    return (jnp.cos(angles).astype(jnp.bfloat16), jnp.sin(angles).astype(jnp.bfloat16))


def local(green_ret, broadening, occupation, neighbours, orbitals, coupling, phonon, mode_table):
    highest = lax.Precision.HIGHEST
    greens = green_ret[0]
    energy_dev = greens.shape[0]
    mixing = jnp.stack(
        [
            jnp.concatenate([broadening[0], broadening[1]], axis=1),
            jnp.concatenate([-broadening[1], broadening[0]], axis=1),
        ],
        axis=0,
    )
    left = jnp.einsum("elpik,pkq->eliq", greens, mixing, preferred_element_type=jnp.float32).astype(
        jnp.bfloat16
    )
    slot_atoms = neighbours % ATL
    selector = slot_atoms[:, :, None] == jnp.arange(ATL, dtype=jnp.int32)[None, None, :]
    layer_orbitals = jnp.repeat(orbitals.reshape(LAYERS, ATL), ATL, axis=0)
    partner_count = jnp.sum(jnp.where(selector, layer_orbitals[:, None, :], 0), axis=2)
    green_rows = greens.reshape(energy_dev, LAYERS, 2, ATL, NORB, ORB)
    select_bf = selector.reshape(LAYERS, ATL, NBR, ATL).astype(jnp.bfloat16)
    partner_rows = jnp.einsum(
        "ljnm,elpmic->eljnpic", select_bf, green_rows, preferred_element_type=jnp.float32
    ).astype(jnp.bfloat16)
    partner_re = partner_rows[:, :, :, :, 0]
    partner_im = partner_rows[:, :, :, :, 1]
    left_rows_re = left[..., :ORB].reshape(energy_dev, LAYERS, ATL, NORB, ORB)
    left_rows_im = left[..., ORB:].reshape(energy_dev, LAYERS, ATL, NORB, ORB)
    pair_re = jnp.einsum(
        "eljic,eljnkc->eljnik", left_rows_re, partner_re, preferred_element_type=jnp.float32
    ) + jnp.einsum(
        "eljic,eljnkc->eljnik", left_rows_im, partner_im, preferred_element_type=jnp.float32
    )
    pair_im = jnp.einsum(
        "eljic,eljnkc->eljnik", left_rows_im, partner_re, preferred_element_type=jnp.float32
    ) - jnp.einsum(
        "eljic,eljnkc->eljnik", left_rows_re, partner_im, preferred_element_type=jnp.float32
    )
    chosen = jnp.stack([pair_re, pair_im], axis=4)
    chosen = chosen.reshape(energy_dev, ATOMS, NBR, 2, NORB, NORB)
    counter = jnp.arange(NORB, dtype=jnp.int32)
    row_mask = counter[None, :] < orbitals[:, None]
    column_mask = counter[None, None, :] < partner_count[:, :, None]
    pair_mask = (row_mask[:, None, :, None] & column_mask[:, :, None, :]).astype(jnp.float32)
    scaled = (
        chosen * occupation[0][:, None, None, None, None, None] * pair_mask[None, :, :, None, :, :]
    )
    pair_blocks = scaled.reshape(energy_dev, ATOMS, NBR, 2, PAIR).astype(jnp.bfloat16)
    arrived = lax.all_to_all(pair_blocks, "shard", split_axis=1, concat_axis=0, tiled=True)
    atom_dev = arrived.shape[1]
    mixed_terms = jnp.einsum(
        "eanpx,anxy->eapy", arrived, coupling, preferred_element_type=jnp.float32
    )
    first_atom = lax.axis_index("shard") * atom_dev
    own_orbitals = lax.dynamic_slice_in_dim(orbitals, first_atom, atom_dev)
    pair_index = jnp.arange(PAIR, dtype=jnp.int32)
    own_mask = (
        (pair_index[None, :] // NORB < own_orbitals[:, None])
        & (pair_index[None, :] % NORB < own_orbitals[:, None])
    ).astype(jnp.float32)
    coupled = (mixed_terms * own_mask[None, :, None, :]).astype(jnp.bfloat16)
    cos_table, sin_table = dft_tables(ENERGIES)
    flat_coupled = coupled.reshape(ENERGIES, -1)
    part_cos = jnp.dot(cos_table, flat_coupled, preferred_element_type=jnp.float32).reshape(
        ENERGIES, atom_dev, 2, PAIR
    )
    part_sin = jnp.dot(sin_table, flat_coupled, preferred_element_type=jnp.float32).reshape(
        ENERGIES, atom_dev, 2, PAIR
    )
    time_data = jnp.stack(
        [part_cos[:, :, 0] + part_sin[:, :, 1], part_cos[:, :, 1] - part_sin[:, :, 0]], axis=2
    ).astype(jnp.bfloat16)
    own_momentum = lax.axis_index("mom")
    mode_count = phonon.shape[0]
    mode_ids = jnp.arange(mode_count, dtype=jnp.int32)
    own_modes = lax.dynamic_slice_in_dim(mode_table, own_momentum, 1, 0)[0]
    phonon_flat = phonon.reshape(mode_count, -1)
    received = lax.all_gather(time_data[None], "mom", axis=0, tiled=True)
    row_count = received.shape[0]
    one_hot = (own_modes[:, None] == mode_ids[None, :]).astype(jnp.float32)
    kernel = jnp.dot(one_hot, phonon_flat, precision=highest).reshape(row_count, 2, ENERGIES)
    values = received.astype(jnp.float32)
    kernel_re = kernel[:, 0][:, :, None, None]
    kernel_im = kernel[:, 1][:, :, None, None]
    add_re = jnp.sum(kernel_re * values[:, :, :, 0] - kernel_im * values[:, :, :, 1], axis=0)
    add_im = jnp.sum(kernel_re * values[:, :, :, 1] + kernel_im * values[:, :, :, 0], axis=0)
    summed = jnp.stack([add_re, add_im], axis=2)
    convolved = summed.astype(jnp.bfloat16)
    flat_conv = convolved.reshape(ENERGIES, -1)
    back_cos = jnp.dot(cos_table, flat_conv, preferred_element_type=jnp.float32).reshape(
        ENERGIES, atom_dev, 2, PAIR
    )
    back_sin = jnp.dot(sin_table, flat_conv, preferred_element_type=jnp.float32).reshape(
        ENERGIES, atom_dev, 2, PAIR
    )
    result_re = (back_cos[:, :, 0] - back_sin[:, :, 1]) * (1.0 / ENERGIES)
    result_im = (back_cos[:, :, 1] + back_sin[:, :, 0]) * (1.0 / ENERGIES)
    return jnp.stack([result_re, result_im], axis=2)[None].astype(jnp.bfloat16)


MESH = pl.DeviceIdType.MESH


def phase_plan(atom_dev, shared):
    return [(0, shared)] + [(start, 1) for start in range(shared, atom_dev)]


def fused_kernel(
    phases,
    shard_count,
    mom_count,
    green_hbm,
    broadening_hbm,
    occupation_hbm,
    neighbours_hbm,
    orbitals_hbm,
    coupling_hbm,
    phonon_hbm,
    modes_hbm,
    cos_hbm,
    sin_hbm,
    out_ref,
    broadening_ref,
    occupation_ref,
    neighbours_ref,
    orbitals_ref,
    phonon_ref,
    modes_ref,
    cos_ref,
    sin_ref,
    small_sem,
    green_buf,
    full_buf,
    send_buf,
    recv_buf,
    coupling_buf,
    kernel_buf,
    mixing_ref,
    turn_ref,
    mirror_buf,
    coupled_buf,
    part_buf,
    time_buf,
    green_sem,
    coupling_sem,
    own_sem,
    send_sem,
    recv_sem,
    mom_send_sem,
    mom_recv_sem,
    mirror_sem,
    forward_send_sem,
    forward_recv_sem,
    part_sem,
):
    me = lax.axis_index("shard")
    mom = lax.axis_index("mom")
    layers, energy_dev = green_buf.shape[0], green_buf.shape[1]
    atom_dev = recv_buf.shape[0]
    dev_layer = ATL // atom_dev
    half = layers // 2
    pieces = NORB // 2
    last = len(phases) - 1
    early = min(2, len(phases))
    shared = phases[0][1]
    half_count = shard_count // 2
    my_half = lax.div(me, half_count)
    my_rank = lax.rem(me, half_count)
    mirror = lax.rem(me + half_count, shard_count)
    half_rows = half_count * energy_dev

    def layer_at(step):
        home = lax.div(me, dev_layer)
        side = lax.rem(lax.div(home, half) + 1 + step, 2)
        return side * half + lax.rem(home + lax.div(step, 2), half)

    def green_copy(layer):
        return pltpu.make_async_copy(
            green_hbm.at[:, layer], green_buf.at[layer], green_sem.at[layer]
        )

    def coupling_copy():
        return pltpu.make_async_copy(coupling_hbm, coupling_buf, coupling_sem)

    def mirror_copy():
        return pltpu.make_async_remote_copy(
            src_ref=coupling_hbm.at[mom],
            dst_ref=mirror_buf.at[mom],
            send_sem=mirror_sem.at[0],
            recv_sem=mirror_sem.at[1],
            device_id={"shard": mirror},
            device_id_type=MESH,
        )

    def forward_copy(step, sending):
        source = lax.rem(mom + mom_count - step, mom_count)
        return pltpu.make_async_remote_copy(
            src_ref=mirror_buf.at[mom],
            dst_ref=mirror_buf.at[mom if sending else source],
            send_sem=forward_send_sem.at[step - 1],
            recv_sem=forward_recv_sem.at[step - 1],
            device_id={"mom": lax.rem(mom + step, mom_count)},
            device_id_type=MESH,
        )

    def part_copy(sending):
        origin = my_half if sending else 1 - my_half
        rows = pl.ds(pl.multiple_of(origin * half_rows, half_rows), half_rows)
        return pltpu.make_async_remote_copy(
            src_ref=part_buf,
            dst_ref=coupled_buf.at[:, :, rows],
            send_sem=part_sem.at[0],
            recv_sem=part_sem.at[1],
            device_id={"shard": mirror},
            device_id_type=MESH,
        )

    def route(phase, dest):
        if phase > 0:
            return dest, me
        crossing = lax.rem(my_half + lax.div(dest, half_count), 2)
        target = my_half * half_count + lax.rem(dest, half_count)
        return target, crossing * half_count + my_rank

    def own_copy(phase, dest):
        start, size = phases[phase]
        slot = route(phase, dest)[1]
        crossing = lax.rem(my_half + lax.div(dest, half_count), 2) if phase == 0 else 0
        return pltpu.make_async_copy(
            send_buf.at[pl.ds(dest * atom_dev + start, size)],
            recv_buf.at[pl.ds(start, size), slot],
            own_sem.at[phase + crossing * len(phases)],
        )

    def send_copy(phase, dest):
        start, size = phases[phase]
        target, slot = route(phase, dest)
        return pltpu.make_async_remote_copy(
            src_ref=send_buf.at[pl.ds(dest * atom_dev + start, size)],
            dst_ref=recv_buf.at[pl.ds(start, size), slot],
            send_sem=send_sem.at[phase, dest],
            recv_sem=recv_sem.at[phase, slot],
            device_id={"shard": target},
            device_id_type=MESH,
        )

    def arrive_copy(phase, slot, source):
        start, size = phases[phase]
        return pltpu.make_async_remote_copy(
            src_ref=send_buf.at[pl.ds(source * atom_dev + start, size)],
            dst_ref=recv_buf.at[pl.ds(start, size), slot],
            send_sem=send_sem.at[phase, source],
            recv_sem=recv_sem.at[phase, slot],
            device_id={"shard": source},
            device_id_type=MESH,
        )

    def mom_copy(phase, step, sending):
        start, size = phases[phase]
        dest = lax.rem(mom + step, mom_count)
        source = lax.rem(mom + mom_count - step, mom_count)
        origin = mom if sending else source
        return pltpu.make_async_remote_copy(
            src_ref=time_buf.at[mom, pl.ds(start, size)],
            dst_ref=time_buf.at[origin, pl.ds(start, size)],
            send_sem=mom_send_sem.at[phase, step - 1],
            recv_sem=mom_recv_sem.at[phase, step - 1],
            device_id={"mom": dest},
            device_id_type=MESH,
        )

    small = [
        (broadening_hbm, broadening_ref),
        (occupation_hbm, occupation_ref),
        (neighbours_hbm, neighbours_ref),
        (orbitals_hbm, orbitals_ref),
        (phonon_hbm, phonon_ref),
        (modes_hbm, modes_ref),
        (cos_hbm, cos_ref),
        (sin_hbm, sin_ref),
    ]
    small = [
        pltpu.make_async_copy(source, held, small_sem.at[index])
        for index, (source, held) in enumerate(small)
    ]
    for copy in small[:4]:
        copy.start()
    for step in range(layers):
        green_copy(layer_at(step)).start()
    for copy in small[4:]:
        copy.start()
    coupling_copy().start()

    barrier = pltpu.get_barrier_semaphore()
    for step in range(1, shard_count):
        pl.semaphore_signal(
            barrier,
            inc=1,
            device_id={"shard": lax.rem(me + step, shard_count)},
            device_id_type=MESH,
        )
    for step in range(1, mom_count):
        pl.semaphore_signal(
            barrier,
            inc=1,
            device_id={"mom": lax.rem(mom + step, mom_count)},
            device_id_type=MESH,
        )
    for copy in small[:4]:
        copy.wait()
    mixing_ref[:ORB, :ORB] = broadening_ref[0]
    mixing_ref[:ORB, ORB:] = broadening_ref[1]
    mixing_ref[ORB:, :ORB] = -broadening_ref[1]
    mixing_ref[ORB:, ORB:] = broadening_ref[0]
    pl.semaphore_wait(barrier, shard_count + mom_count - 2)
    mirror_copy().start()
    turn_shape = turn_ref.shape
    wanted = lax.broadcasted_iota(jnp.int32, turn_shape, 0)
    held = lax.broadcasted_iota(jnp.int32, turn_shape, 1)
    wanted = lax.rem(wanted, energy_dev) * NORB + lax.div(wanted, energy_dev)
    turn_ref[...] = jnp.where(wanted == held, 1.0, 0.0).astype(jnp.bfloat16)
    group = 8
    unroll = 4

    def layer_pairs(layer):
        green_copy(layer).wait()

        def energy_step(index, inner):
            first = index * group
            joined = [
                jnp.concatenate(
                    [green_buf[layer, first + j, 0], green_buf[layer, first + j, 1]], axis=1
                )
                for j in range(group)
            ]
            left = jnp.dot(
                jnp.concatenate(joined, axis=0),
                mixing_ref[...],
                preferred_element_type=jnp.float32,
            ).astype(jnp.bfloat16)
            for j in range(group):
                own_left = left[j * ORB : (j + 1) * ORB]
                products = lax.dot_general(
                    jnp.concatenate([own_left[:, :ORB], own_left[:, ORB:]], axis=0),
                    jnp.concatenate([joined[j][:, :ORB], joined[j][:, ORB:]], axis=0),
                    (((1,), (1,)), ((), ())),
                    preferred_element_type=jnp.float32,
                )
                full_re = products[:ORB, :ORB] + products[ORB:, ORB:]
                full_im = products[ORB:, :ORB] - products[:ORB, ORB:]
                weight = occupation_ref[0, first + j]
                full_buf[first + j, :, :ORB] = (full_re * weight).astype(jnp.bfloat16)
                full_buf[first + j, :, ORB:] = (full_im * weight).astype(jnp.bfloat16)
            return inner

        lax.fori_loop(0, energy_dev // group, energy_step, 0)

        lane = lax.broadcasted_iota(jnp.int32, (1, ORB), 1)
        lane_slot = lax.rem(lax.div(lane, NORB), NBR)
        lane_base = lax.rem(lane, NORB) + lax.div(lane, NORB * NBR) * ORB
        row_ids = lax.broadcasted_iota(jnp.int32, (2 * ORB, ORB), 0)

        def pick_atom(slot):
            atom = layer * ATL + slot
            target = lane_base
            for near in range(NBR):
                start = (neighbours_ref[near, atom] - layer * ATL) * NORB
                target = target + jnp.where(lane_slot == near, start, 0)
            rows = pl.ds(pl.multiple_of(slot * NORB, NORB), NORB)
            block = full_buf[:, rows, :].reshape(energy_dev * NORB, 2 * ORB)
            turned = jnp.dot(
                turn_ref[...], block, preferred_element_type=jnp.float32
            ).astype(jnp.bfloat16)
            strips = []
            for part in range(2):
                columns = slice(part * ORB, (part + 1) * ORB)
                for piece in range(pieces):
                    begin = 2 * piece * energy_dev
                    pair = [
                        turned[begin + low * energy_dev : begin + (low + 1) * energy_dev, columns]
                        for low in range(2)
                    ]
                    strips.append(jnp.concatenate(pair, axis=1))
            stacked = jnp.concatenate(strips, axis=0)
            chosen = jnp.where(row_ids == target, 1.0, 0.0)
            picked = jnp.dot(
                stacked, chosen.astype(jnp.bfloat16), preferred_element_type=jnp.float32
            )
            send_buf[atom] = picked.astype(jnp.bfloat16).reshape(2 * pieces, energy_dev, ORB)

        def atom_step(index, inner):
            for j in range(unroll):
                pick_atom(index * unroll + j)
            return inner

        lax.fori_loop(0, ATL // unroll, atom_step, 0)

    def layer_step(step, carry):
        layer_pairs(layer_at(step))
        for phase in range(early):
            start_sends(phase, layer_at(step))

        @pl.when(step == layers - 2)
        def _():
            mirror_copy().wait_recv()
            for other in range(1, mom_count):
                forward_copy(other, True).start()

        return carry

    def mask_coupling(buffer, atom, place):
        shape = (NORB, PAIR)
        column = lax.broadcasted_iota(jnp.int32, shape, 0)
        entry = lax.broadcasted_iota(jnp.int32, shape, 1)
        outer, inner = lax.div(entry, NORB), lax.rem(entry, NORB)
        own = orbitals_ref[place]
        kept = (outer < own) & (inner < own)
        masks = [
            jnp.where(kept & (column < orbitals_ref[neighbours_ref[near, place]]), 1.0, 0.0)
            for near in range(NBR)
        ]

        def row_step(row, carry):
            used = jnp.where(row < own, 1.0, 0.0)
            for near in range(NBR):
                block = buffer[atom, near, row].astype(jnp.float32)
                buffer[atom, near, row] = (block * (masks[near] * used)).astype(jnp.bfloat16)
            return carry

        lax.fori_loop(0, NORB, row_step, 0)

    def spread_phonon():
        for other in range(mom_count):
            mode = modes_ref[mom, other]
            rows = phonon_ref[mode]
            for part in range(2):
                wide = jnp.broadcast_to(rows[part : part + 1], (ORB, rows.shape[1]))
                kernel_buf[other, part] = wide.T

    def start_sends(phase, layer):
        for offset in range(dev_layer):
            dest = layer * dev_layer + offset
            if phase >= early:
                before = phase - early

                @pl.when(route(before, dest)[0] != me)
                def _():
                    send_copy(before, dest).wait_send()

            target = route(phase, dest)[0]

            @pl.when(target != me)
            def _():
                send_copy(phase, dest).start()

            @pl.when(target == me)
            def _():
                own_copy(phase, dest).start()

    def finish(phase):
        start, size = phases[phase]
        for step in range(1, mom_count):
            mom_copy(phase, step, False).wait_recv()
        for atom in range(start, start + size):
            sums = [0.0, 0.0]
            for other in range(mom_count):
                wide_re = jnp.concatenate([kernel_buf[other, 0]] * (PAIR // ORB), axis=1)
                wide_im = jnp.concatenate([kernel_buf[other, 1]] * (PAIR // ORB), axis=1)
                time_re = time_buf[other, atom, 0].astype(jnp.float32)
                time_im = time_buf[other, atom, 1].astype(jnp.float32)
                sums[0] = sums[0] + (wide_re * time_re - wide_im * time_im)
                sums[1] = sums[1] + (wide_re * time_im + wide_im * time_re)
            conv_re = sums[0].astype(jnp.bfloat16)
            conv_im = sums[1].astype(jnp.bfloat16)
            scale = 1.0 / cos_ref.shape[0]
            res_re = (dot(cos_ref[...], conv_re) - dot(sin_ref[...], conv_im)) * scale
            res_im = (dot(cos_ref[...], conv_im) + dot(sin_ref[...], conv_re)) * scale
            base = atom * 2 * PAIR
            out_ref[:, base : base + PAIR] = res_re.astype(jnp.bfloat16)
            out_ref[:, base + PAIR : base + 2 * PAIR] = res_im.astype(jnp.bfloat16)

    dot = functools.partial(jnp.dot, preferred_element_type=jnp.float32)

    def arrive_all(phase):
        def arrive(slot, carry):
            source = slot
            if phase == 0:
                source = my_half * half_count + lax.rem(slot, half_count)

            @pl.when(source != me)
            def _():
                arrive_copy(phase, slot, source).wait_recv()

            return carry

        lax.fori_loop(0, shard_count, arrive, 0)
        own_copy(phase, me).wait()
        if phase == 0:
            own_copy(phase, mirror).wait()

    def couple(atom, weights, place, first, count):
        result = []
        for part in range(2):
            total = 0.0
            for piece in range(0, pieces, 2):
                block = jnp.concatenate(
                    [
                        recv_buf[
                            atom, first : first + count, part * pieces + piece + low
                        ].reshape(count * energy_dev, ORB)
                        for low in range(2)
                    ],
                    axis=1,
                )
                matrix = jnp.concatenate(
                    [
                        weights[place, near, row]
                        for row in range(2 * piece, 2 * piece + 4)
                        for near in range(NBR)
                    ],
                    axis=0,
                )
                total = total + dot(block, matrix)
            result.append(total.astype(jnp.bfloat16))
        return result

    def to_time(atom, coupled):
        time_re = dot(cos_ref[...], coupled[0]) + dot(sin_ref[...], coupled[1])
        time_im = dot(cos_ref[...], coupled[1]) - dot(sin_ref[...], coupled[0])
        time_buf[mom, atom, 0] = time_re.astype(jnp.bfloat16)
        time_buf[mom, atom, 1] = time_im.astype(jnp.bfloat16)

    def mirror_part():
        for other in range(1, mom_count):
            forward_copy(other, True).wait_send()
            forward_copy(other, False).wait_recv()
        for atom in range(shared):
            mask_coupling(mirror_buf, atom, mirror * atom_dev + atom)
        arrive_all(0)
        for atom in range(shared):
            far = couple(atom, mirror_buf, atom, half_count, half_count)
            for part in range(2):
                part_buf[atom, part] = far[part]
        part_copy(True).start()
        rows = pl.ds(pl.multiple_of(my_half * half_rows, half_rows), half_rows)
        for atom in range(shared):
            near = couple(atom, coupling_buf, atom, 0, half_count)
            for part in range(2):
                coupled_buf[atom, part, rows, :] = near[part]

    def transform(phase):
        start, size = phases[phase]
        if phase == 0:
            mirror_part()
            part_copy(False).wait_recv()
            for atom in range(size):
                to_time(atom, [coupled_buf[atom, 0], coupled_buf[atom, 1]])
        else:
            arrive_all(phase)
            for atom in range(start, start + size):
                to_time(atom, couple(atom, coupling_buf, atom, 0, shard_count))
        for step in range(1, mom_count):
            mom_copy(phase, step, True).start()

    lax.fori_loop(0, layers, layer_step, 0)
    for copy in small[4:]:
        copy.wait()
    coupling_copy().wait()
    for atom in range(atom_dev):
        mask_coupling(coupling_buf, atom, me * atom_dev + atom)
    spread_phonon()

    def send_phase(phase):
        def more(step, carry):
            start_sends(phase, layer_at(step))
            return carry

        lax.fori_loop(0, layers, more, 0)

    done = 0
    for phase in range(len(phases)):
        if phase + 2 <= last and phase + 2 >= early:
            send_phase(phase + 2)
        transform(phase)
        if phase >= 2 or phase == last:
            while done < phase:
                finish(done)
                done += 1
        elif phase == 1:
            finish(0)
            done = 1
    finish(last)

    def drain(dest, carry):
        for phase in range(max(len(phases) - early, 0), len(phases)):

            @pl.when(route(phase, dest)[0] != me)
            def _():
                send_copy(phase, dest).wait_send()

        return carry

    lax.fori_loop(0, shard_count, drain, 0)
    mirror_copy().wait_send()
    part_copy(True).wait_send()
    for phase in range(len(phases)):
        for step in range(1, mom_count):
            mom_copy(phase, step, True).wait_send()


def fused(shard_count, mom_count, green_ret, broadening, occupation, neighbours, orbitals,
          coupling, phonon, mode_table):
    greens = green_ret[0]
    energy_dev = greens.shape[0]
    atom_dev = coupling.shape[0]
    energies = phonon.shape[-1]
    counter = np.arange(energies, dtype=np.int32)
    angles = (counter[:, None] * counter[None, :] % energies).astype(np.float32)
    angles = angles * np.float32(2.0 * math.pi / energies)
    cos_table = jnp.asarray(np.cos(angles), jnp.bfloat16)
    sin_table = jnp.asarray(np.sin(angles), jnp.bfloat16)
    blocks = coupling.reshape(atom_dev, NBR, NORB, NORB, PAIR)
    shared = mom_count
    phases = phase_plan(atom_dev, shared)
    count = len(phases)
    vmem = pl.BlockSpec(memory_space=pltpu.VMEM)
    hbm = pl.BlockSpec(memory_space=pl.ANY)
    smem = pltpu.SMEM
    dma = pltpu.SemaphoreType.DMA
    result = pl.pallas_call(
        functools.partial(fused_kernel, phases, shard_count, mom_count),
        out_shape=jax.ShapeDtypeStruct((energies, atom_dev * 2 * PAIR), jnp.bfloat16),
        in_specs=[hbm] * 10,
        out_specs=vmem,
        scratch_shapes=[
            pltpu.VMEM(broadening.shape, broadening.dtype),
            smem(occupation.shape, occupation.dtype),
            smem(neighbours.shape[::-1], neighbours.dtype),
            smem(orbitals.shape, orbitals.dtype),
            pltpu.VMEM(phonon.shape, phonon.dtype),
            smem(mode_table.shape, mode_table.dtype),
            pltpu.VMEM(cos_table.shape, cos_table.dtype),
            pltpu.VMEM(sin_table.shape, sin_table.dtype),
            dma((8,)),
            pltpu.VMEM((LAYERS, energy_dev, 2, ORB, ORB), jnp.bfloat16),
            pltpu.VMEM((energy_dev, ORB, 2 * ORB), jnp.bfloat16),
            pltpu.VMEM((ATOMS, NORB, energy_dev, ORB), jnp.bfloat16),
            pltpu.VMEM((atom_dev, shard_count, NORB, energy_dev, ORB), jnp.bfloat16),
            pltpu.VMEM((atom_dev, NBR, NORB, NORB, PAIR), jnp.bfloat16),
            pltpu.VMEM((mom_count, 2, energies, ORB), jnp.float32),
            pltpu.VMEM((2 * ORB, 2 * ORB), jnp.bfloat16),
            pltpu.VMEM((energy_dev * NORB, energy_dev * NORB), jnp.bfloat16),
            pltpu.VMEM((shared, NBR, NORB, NORB, PAIR), jnp.bfloat16),
            pltpu.VMEM((shared, 2, energies, PAIR), jnp.bfloat16),
            pltpu.VMEM((shared, 2, energies // 2, PAIR), jnp.bfloat16),
            pltpu.VMEM((mom_count, atom_dev, 2, energies, PAIR), jnp.bfloat16),
            dma((LAYERS,)),
            dma,
            dma((2 * count,)),
            dma((count, shard_count)),
            dma((count, shard_count)),
            dma((count, max(mom_count - 1, 1))),
            dma((count, max(mom_count - 1, 1))),
            dma((2,)),
            dma((max(mom_count - 1, 1),)),
            dma((max(mom_count - 1, 1),)),
            dma((2,)),
        ],
        compiler_params=pltpu.CompilerParams(
            collective_id=0, has_side_effects=True, vmem_limit_bytes=56 * 1024 * 1024
        ),
    )(
        greens, broadening, occupation, neighbours.T, orbitals, blocks, phonon, mode_table,
        cos_table, sin_table,
    )
    return result.reshape(1, energies, atom_dev, 2, PAIR)


def solution(mesh):
    in_specs = (
        P("mom", "shard", None, None, None, None),
        P(),
        P("mom", "shard"),
        P(),
        P(),
        P("shard", None, None, None),
        P(),
        P(),
    )
    out_specs = P("mom", None, "shard", None, None)
    shard_count, mom_count = mesh.shape["shard"], mesh.shape["mom"]

    def body(*args):
        energy_dev, atom_dev = args[0].shape[1], args[5].shape[0]
        if energy_dev % 16 == 0 and ATL % atom_dev == 0 and atom_dev >= mom_count + 2:
            return fused(shard_count, mom_count, *args)
        return local(*args)

    return jax.shard_map(body, mesh=mesh, in_specs=in_specs, out_specs=out_specs, check_vma=False)
```

```python
import functools
import math

import jax
import jax.numpy as jnp
import numpy as np
from jax import lax
from jax.experimental import pallas as pl
from jax.experimental.pallas import tpu as pltpu
from jax.sharding import PartitionSpec as P

NORB = 16
ATL = 8
NBR = 4
ENERGIES = 256
LAYERS = 8
ORB = 128
PAIR = 256
ATOMS = 64


def dft_tables(length):
    counter = jnp.arange(length, dtype=jnp.int32)
    phases = counter[:, None] * counter[None, :] % length
    angles = phases.astype(jnp.float32) * (2.0 * math.pi / length)
    return (jnp.cos(angles).astype(jnp.bfloat16), jnp.sin(angles).astype(jnp.bfloat16))


def local(green_ret, broadening, occupation, neighbours, orbitals, coupling, phonon, mode_table):
    highest = lax.Precision.HIGHEST
    greens = green_ret[0]
    energy_dev = greens.shape[0]
    mixing = jnp.stack(
        [
            jnp.concatenate([broadening[0], broadening[1]], axis=1),
            jnp.concatenate([-broadening[1], broadening[0]], axis=1),
        ],
        axis=0,
    )
    left = jnp.einsum("elpik,pkq->eliq", greens, mixing, preferred_element_type=jnp.float32).astype(
        jnp.bfloat16
    )
    slot_atoms = neighbours % ATL
    selector = slot_atoms[:, :, None] == jnp.arange(ATL, dtype=jnp.int32)[None, None, :]
    layer_orbitals = jnp.repeat(orbitals.reshape(LAYERS, ATL), ATL, axis=0)
    partner_count = jnp.sum(jnp.where(selector, layer_orbitals[:, None, :], 0), axis=2)
    green_rows = greens.reshape(energy_dev, LAYERS, 2, ATL, NORB, ORB)
    select_bf = selector.reshape(LAYERS, ATL, NBR, ATL).astype(jnp.bfloat16)
    partner_rows = jnp.einsum(
        "ljnm,elpmic->eljnpic", select_bf, green_rows, preferred_element_type=jnp.float32
    ).astype(jnp.bfloat16)
    partner_re = partner_rows[:, :, :, :, 0]
    partner_im = partner_rows[:, :, :, :, 1]
    left_rows_re = left[..., :ORB].reshape(energy_dev, LAYERS, ATL, NORB, ORB)
    left_rows_im = left[..., ORB:].reshape(energy_dev, LAYERS, ATL, NORB, ORB)
    pair_re = jnp.einsum(
        "eljic,eljnkc->eljnik", left_rows_re, partner_re, preferred_element_type=jnp.float32
    ) + jnp.einsum(
        "eljic,eljnkc->eljnik", left_rows_im, partner_im, preferred_element_type=jnp.float32
    )
    pair_im = jnp.einsum(
        "eljic,eljnkc->eljnik", left_rows_im, partner_re, preferred_element_type=jnp.float32
    ) - jnp.einsum(
        "eljic,eljnkc->eljnik", left_rows_re, partner_im, preferred_element_type=jnp.float32
    )
    chosen = jnp.stack([pair_re, pair_im], axis=4)
    chosen = chosen.reshape(energy_dev, ATOMS, NBR, 2, NORB, NORB)
    counter = jnp.arange(NORB, dtype=jnp.int32)
    row_mask = counter[None, :] < orbitals[:, None]
    column_mask = counter[None, None, :] < partner_count[:, :, None]
    pair_mask = (row_mask[:, None, :, None] & column_mask[:, :, None, :]).astype(jnp.float32)
    scaled = (
        chosen * occupation[0][:, None, None, None, None, None] * pair_mask[None, :, :, None, :, :]
    )
    pair_blocks = scaled.reshape(energy_dev, ATOMS, NBR, 2, PAIR).astype(jnp.bfloat16)
    arrived = lax.all_to_all(pair_blocks, "shard", split_axis=1, concat_axis=0, tiled=True)
    atom_dev = arrived.shape[1]
    mixed_terms = jnp.einsum(
        "eanpx,anxy->eapy", arrived, coupling, preferred_element_type=jnp.float32
    )
    first_atom = lax.axis_index("shard") * atom_dev
    own_orbitals = lax.dynamic_slice_in_dim(orbitals, first_atom, atom_dev)
    pair_index = jnp.arange(PAIR, dtype=jnp.int32)
    own_mask = (
        (pair_index[None, :] // NORB < own_orbitals[:, None])
        & (pair_index[None, :] % NORB < own_orbitals[:, None])
    ).astype(jnp.float32)
    coupled = (mixed_terms * own_mask[None, :, None, :]).astype(jnp.bfloat16)
    cos_table, sin_table = dft_tables(ENERGIES)
    flat_coupled = coupled.reshape(ENERGIES, -1)
    part_cos = jnp.dot(cos_table, flat_coupled, preferred_element_type=jnp.float32).reshape(
        ENERGIES, atom_dev, 2, PAIR
    )
    part_sin = jnp.dot(sin_table, flat_coupled, preferred_element_type=jnp.float32).reshape(
        ENERGIES, atom_dev, 2, PAIR
    )
    time_data = jnp.stack(
        [part_cos[:, :, 0] + part_sin[:, :, 1], part_cos[:, :, 1] - part_sin[:, :, 0]], axis=2
    ).astype(jnp.bfloat16)
    own_momentum = lax.axis_index("mom")
    mode_count = phonon.shape[0]
    mode_ids = jnp.arange(mode_count, dtype=jnp.int32)
    own_modes = lax.dynamic_slice_in_dim(mode_table, own_momentum, 1, 0)[0]
    phonon_flat = phonon.reshape(mode_count, -1)
    received = lax.all_gather(time_data[None], "mom", axis=0, tiled=True)
    row_count = received.shape[0]
    one_hot = (own_modes[:, None] == mode_ids[None, :]).astype(jnp.float32)
    kernel = jnp.dot(one_hot, phonon_flat, precision=highest).reshape(row_count, 2, ENERGIES)
    values = received.astype(jnp.float32)
    kernel_re = kernel[:, 0][:, :, None, None]
    kernel_im = kernel[:, 1][:, :, None, None]
    add_re = jnp.sum(kernel_re * values[:, :, :, 0] - kernel_im * values[:, :, :, 1], axis=0)
    add_im = jnp.sum(kernel_re * values[:, :, :, 1] + kernel_im * values[:, :, :, 0], axis=0)
    summed = jnp.stack([add_re, add_im], axis=2)
    convolved = summed.astype(jnp.bfloat16)
    flat_conv = convolved.reshape(ENERGIES, -1)
    back_cos = jnp.dot(cos_table, flat_conv, preferred_element_type=jnp.float32).reshape(
        ENERGIES, atom_dev, 2, PAIR
    )
    back_sin = jnp.dot(sin_table, flat_conv, preferred_element_type=jnp.float32).reshape(
        ENERGIES, atom_dev, 2, PAIR
    )
    result_re = (back_cos[:, :, 0] - back_sin[:, :, 1]) * (1.0 / ENERGIES)
    result_im = (back_cos[:, :, 1] + back_sin[:, :, 0]) * (1.0 / ENERGIES)
    return jnp.stack([result_re, result_im], axis=2)[None].astype(jnp.bfloat16)


MESH = pl.DeviceIdType.MESH


def phase_plan(atom_dev, shared):
    return [(0, shared)] + [(start, 1) for start in range(shared, atom_dev)]


def fused_kernel(
    phases,
    shard_count,
    mom_count,
    green_hbm,
    broadening_hbm,
    occupation_hbm,
    neighbours_hbm,
    orbitals_hbm,
    coupling_hbm,
    phonon_hbm,
    modes_hbm,
    cos_hbm,
    sin_hbm,
    out_ref,
    broadening_ref,
    occupation_ref,
    neighbours_ref,
    orbitals_ref,
    phonon_ref,
    modes_ref,
    cos_ref,
    sin_ref,
    small_sem,
    green_buf,
    full_buf,
    send_buf,
    recv_buf,
    coupling_buf,
    kernel_buf,
    mixing_ref,
    turn_ref,
    mirror_buf,
    coupled_buf,
    part_buf,
    time_buf,
    green_sem,
    coupling_sem,
    own_sem,
    send_sem,
    recv_sem,
    mom_send_sem,
    mom_recv_sem,
    mirror_sem,
    forward_send_sem,
    forward_recv_sem,
    part_sem,
):
    me = lax.axis_index("shard")
    mom = lax.axis_index("mom")
    layers, energy_dev = green_buf.shape[0], green_buf.shape[1]
    atom_dev = recv_buf.shape[0]
    dev_layer = ATL // atom_dev
    half = layers // 2
    pieces = NORB // 2
    last = len(phases) - 1
    early = min(2, len(phases))
    shared = phases[0][1]
    half_count = shard_count // 2
    my_half = lax.div(me, half_count)
    my_rank = lax.rem(me, half_count)
    mirror = lax.rem(me + half_count, shard_count)
    half_rows = half_count * energy_dev

    def layer_at(step):
        home = lax.div(me, dev_layer)
        side = lax.rem(lax.div(home, half) + 1 + step, 2)
        return side * half + lax.rem(home + lax.div(step, 2), half)

    def green_copy(layer):
        return pltpu.make_async_copy(
            green_hbm.at[:, layer], green_buf.at[layer], green_sem.at[layer]
        )

    def coupling_copy():
        return pltpu.make_async_copy(coupling_hbm, coupling_buf, coupling_sem)

    def mirror_copy():
        return pltpu.make_async_remote_copy(
            src_ref=coupling_hbm.at[mom],
            dst_ref=mirror_buf.at[mom],
            send_sem=mirror_sem.at[0],
            recv_sem=mirror_sem.at[1],
            device_id={"shard": mirror},
            device_id_type=MESH,
        )

    def forward_copy(step, sending):
        source = lax.rem(mom + mom_count - step, mom_count)
        return pltpu.make_async_remote_copy(
            src_ref=mirror_buf.at[mom],
            dst_ref=mirror_buf.at[mom if sending else source],
            send_sem=forward_send_sem.at[step - 1],
            recv_sem=forward_recv_sem.at[step - 1],
            device_id={"mom": lax.rem(mom + step, mom_count)},
            device_id_type=MESH,
        )

    def part_copy(sending):
        origin = my_half if sending else 1 - my_half
        rows = pl.ds(pl.multiple_of(origin * half_rows, half_rows), half_rows)
        return pltpu.make_async_remote_copy(
            src_ref=part_buf,
            dst_ref=coupled_buf.at[:, :, rows],
            send_sem=part_sem.at[0],
            recv_sem=part_sem.at[1],
            device_id={"shard": mirror},
            device_id_type=MESH,
        )

    def route(phase, dest):
        if phase > 0:
            return dest, me
        crossing = lax.rem(my_half + lax.div(dest, half_count), 2)
        target = my_half * half_count + lax.rem(dest, half_count)
        return target, crossing * half_count + my_rank

    def own_copy(phase, dest):
        start, size = phases[phase]
        slot = route(phase, dest)[1]
        crossing = lax.rem(my_half + lax.div(dest, half_count), 2) if phase == 0 else 0
        return pltpu.make_async_copy(
            send_buf.at[pl.ds(dest * atom_dev + start, size)],
            recv_buf.at[pl.ds(start, size), slot],
            own_sem.at[phase + crossing * len(phases)],
        )

    def send_copy(phase, dest):
        start, size = phases[phase]
        target, slot = route(phase, dest)
        return pltpu.make_async_remote_copy(
            src_ref=send_buf.at[pl.ds(dest * atom_dev + start, size)],
            dst_ref=recv_buf.at[pl.ds(start, size), slot],
            send_sem=send_sem.at[phase, dest],
            recv_sem=recv_sem.at[phase, slot],
            device_id={"shard": target},
            device_id_type=MESH,
        )

    def arrive_copy(phase, slot, source):
        start, size = phases[phase]
        return pltpu.make_async_remote_copy(
            src_ref=send_buf.at[pl.ds(source * atom_dev + start, size)],
            dst_ref=recv_buf.at[pl.ds(start, size), slot],
            send_sem=send_sem.at[phase, source],
            recv_sem=recv_sem.at[phase, slot],
            device_id={"shard": source},
            device_id_type=MESH,
        )

    def mom_copy(phase, step, sending):
        start, size = phases[phase]
        dest = lax.rem(mom + step, mom_count)
        source = lax.rem(mom + mom_count - step, mom_count)
        origin = mom if sending else source
        return pltpu.make_async_remote_copy(
            src_ref=time_buf.at[mom, pl.ds(start, size)],
            dst_ref=time_buf.at[origin, pl.ds(start, size)],
            send_sem=mom_send_sem.at[phase, step - 1],
            recv_sem=mom_recv_sem.at[phase, step - 1],
            device_id={"mom": dest},
            device_id_type=MESH,
        )

    small = [
        (broadening_hbm, broadening_ref),
        (occupation_hbm, occupation_ref),
        (neighbours_hbm, neighbours_ref),
        (orbitals_hbm, orbitals_ref),
        (phonon_hbm, phonon_ref),
        (modes_hbm, modes_ref),
        (cos_hbm, cos_ref),
        (sin_hbm, sin_ref),
    ]
    small = [
        pltpu.make_async_copy(source, held, small_sem.at[index])
        for index, (source, held) in enumerate(small)
    ]
    for copy in small[:4]:
        copy.start()
    for step in range(layers):
        green_copy(layer_at(step)).start()
    for copy in small[4:]:
        copy.start()
    coupling_copy().start()

    barrier = pltpu.get_barrier_semaphore()
    for step in range(1, shard_count):
        pl.semaphore_signal(
            barrier,
            inc=1,
            device_id={"shard": lax.rem(me + step, shard_count)},
            device_id_type=MESH,
        )
    for step in range(1, mom_count):
        pl.semaphore_signal(
            barrier,
            inc=1,
            device_id={"mom": lax.rem(mom + step, mom_count)},
            device_id_type=MESH,
        )
    for copy in small[:4]:
        copy.wait()
    mixing_ref[:ORB, :ORB] = broadening_ref[0]
    mixing_ref[:ORB, ORB:] = broadening_ref[1]
    mixing_ref[ORB:, :ORB] = -broadening_ref[1]
    mixing_ref[ORB:, ORB:] = broadening_ref[0]
    pl.semaphore_wait(barrier, shard_count + mom_count - 2)
    mirror_copy().start()
    turn_shape = turn_ref.shape
    wanted = lax.broadcasted_iota(jnp.int32, turn_shape, 0)
    held = lax.broadcasted_iota(jnp.int32, turn_shape, 1)
    wanted = lax.rem(wanted, energy_dev) * NORB + lax.div(wanted, energy_dev)
    turn_ref[...] = jnp.where(wanted == held, 1.0, 0.0).astype(jnp.bfloat16)
    group = 8
    unroll = 4

    def layer_pairs(layer):
        green_copy(layer).wait()

        def energy_step(index, inner):
            first = index * group
            joined = [
                jnp.concatenate(
                    [green_buf[layer, first + j, 0], green_buf[layer, first + j, 1]], axis=1
                )
                for j in range(group)
            ]
            left = jnp.dot(
                jnp.concatenate(joined, axis=0),
                mixing_ref[...],
                preferred_element_type=jnp.float32,
            ).astype(jnp.bfloat16)
            for j in range(group):
                own_left = left[j * ORB : (j + 1) * ORB]
                products = lax.dot_general(
                    jnp.concatenate([own_left[:, :ORB], own_left[:, ORB:]], axis=0),
                    jnp.concatenate([joined[j][:, :ORB], joined[j][:, ORB:]], axis=0),
                    (((1,), (1,)), ((), ())),
                    preferred_element_type=jnp.float32,
                )
                full_re = products[:ORB, :ORB] + products[ORB:, ORB:]
                full_im = products[ORB:, :ORB] - products[:ORB, ORB:]
                weight = occupation_ref[0, first + j]
                full_buf[first + j, :, :ORB] = (full_re * weight).astype(jnp.bfloat16)
                full_buf[first + j, :, ORB:] = (full_im * weight).astype(jnp.bfloat16)
            return inner

        lax.fori_loop(0, energy_dev // group, energy_step, 0)

        lane = lax.broadcasted_iota(jnp.int32, (1, ORB), 1)
        lane_slot = lax.rem(lax.div(lane, NORB), NBR)
        lane_base = lax.rem(lane, NORB) + lax.div(lane, NORB * NBR) * ORB
        row_ids = lax.broadcasted_iota(jnp.int32, (2 * ORB, ORB), 0)

        def pick_atom(slot):
            atom = layer * ATL + slot
            target = lane_base
            for near in range(NBR):
                start = (neighbours_ref[near, atom] - layer * ATL) * NORB
                target = target + jnp.where(lane_slot == near, start, 0)
            rows = pl.ds(pl.multiple_of(slot * NORB, NORB), NORB)
            block = full_buf[:, rows, :].reshape(energy_dev * NORB, 2 * ORB)
            turned = jnp.dot(
                turn_ref[...], block, preferred_element_type=jnp.float32
            ).astype(jnp.bfloat16)
            strips = []
            for part in range(2):
                columns = slice(part * ORB, (part + 1) * ORB)
                for piece in range(pieces):
                    begin = 2 * piece * energy_dev
                    pair = [
                        turned[begin + low * energy_dev : begin + (low + 1) * energy_dev, columns]
                        for low in range(2)
                    ]
                    strips.append(jnp.concatenate(pair, axis=1))
            stacked = jnp.concatenate(strips, axis=0)
            chosen = jnp.where(row_ids == target, 1.0, 0.0)
            picked = jnp.dot(
                stacked, chosen.astype(jnp.bfloat16), preferred_element_type=jnp.float32
            )
            send_buf[atom] = picked.astype(jnp.bfloat16).reshape(2 * pieces, energy_dev, ORB)

        def atom_step(index, inner):
            for j in range(unroll):
                pick_atom(index * unroll + j)
            return inner

        lax.fori_loop(0, ATL // unroll, atom_step, 0)

    def layer_step(step, carry):
        layer_pairs(layer_at(step))
        for phase in range(early):
            start_sends(phase, layer_at(step))

        @pl.when(step == layers - 2)
        def _():
            mirror_copy().wait_recv()
            for other in range(1, mom_count):
                forward_copy(other, True).start()

        return carry

    def mask_coupling(buffer, atom, place):
        shape = (NORB, PAIR)
        column = lax.broadcasted_iota(jnp.int32, shape, 0)
        entry = lax.broadcasted_iota(jnp.int32, shape, 1)
        outer, inner = lax.div(entry, NORB), lax.rem(entry, NORB)
        own = orbitals_ref[place]
        kept = (outer < own) & (inner < own)
        masks = [
            jnp.where(kept & (column < orbitals_ref[neighbours_ref[near, place]]), 1.0, 0.0)
            for near in range(NBR)
        ]

        def row_step(row, carry):
            used = jnp.where(row < own, 1.0, 0.0)
            for near in range(NBR):
                block = buffer[atom, near, row].astype(jnp.float32)
                buffer[atom, near, row] = (block * (masks[near] * used)).astype(jnp.bfloat16)
            return carry

        lax.fori_loop(0, NORB, row_step, 0)

    def spread_phonon():
        for other in range(mom_count):
            mode = modes_ref[mom, other]
            rows = phonon_ref[mode]
            for part in range(2):
                wide = jnp.broadcast_to(rows[part : part + 1], (ORB, rows.shape[1]))
                kernel_buf[other, part] = wide.T

    def start_sends(phase, layer):
        for offset in range(dev_layer):
            dest = layer * dev_layer + offset
            if phase >= early:
                before = phase - early

                @pl.when(route(before, dest)[0] != me)
                def _():
                    send_copy(before, dest).wait_send()

            target = route(phase, dest)[0]

            @pl.when(target != me)
            def _():
                send_copy(phase, dest).start()

            @pl.when(target == me)
            def _():
                own_copy(phase, dest).start()

    def finish(phase):
        start, size = phases[phase]
        for step in range(1, mom_count):
            mom_copy(phase, step, False).wait_recv()
        for atom in range(start, start + size):
            sums = [0.0, 0.0]
            for other in range(mom_count):
                wide_re = jnp.concatenate([kernel_buf[other, 0]] * (PAIR // ORB), axis=1)
                wide_im = jnp.concatenate([kernel_buf[other, 1]] * (PAIR // ORB), axis=1)
                time_re = time_buf[other, atom, 0].astype(jnp.float32)
                time_im = time_buf[other, atom, 1].astype(jnp.float32)
                sums[0] = sums[0] + (wide_re * time_re - wide_im * time_im)
                sums[1] = sums[1] + (wide_re * time_im + wide_im * time_re)
            conv_re = sums[0].astype(jnp.bfloat16)
            conv_im = sums[1].astype(jnp.bfloat16)
            scale = 1.0 / cos_ref.shape[0]
            res_re = (dot(cos_ref[...], conv_re) - dot(sin_ref[...], conv_im)) * scale
            res_im = (dot(cos_ref[...], conv_im) + dot(sin_ref[...], conv_re)) * scale
            base = atom * 2 * PAIR
            out_ref[:, base : base + PAIR] = res_re.astype(jnp.bfloat16)
            out_ref[:, base + PAIR : base + 2 * PAIR] = res_im.astype(jnp.bfloat16)

    dot = functools.partial(jnp.dot, preferred_element_type=jnp.float32)

    def arrive_all(phase):
        def arrive(slot, carry):
            source = slot
            if phase == 0:
                source = my_half * half_count + lax.rem(slot, half_count)

            @pl.when(source != me)
            def _():
                arrive_copy(phase, slot, source).wait_recv()

            return carry

        lax.fori_loop(0, shard_count, arrive, 0)
        own_copy(phase, me).wait()
        if phase == 0:
            own_copy(phase, mirror).wait()

    def couple(atom, weights, place, first, count):
        result = []
        for part in range(2):
            total = 0.0
            for piece in range(0, pieces, 2):
                block = jnp.concatenate(
                    [
                        recv_buf[
                            atom, first : first + count, part * pieces + piece + low
                        ].reshape(count * energy_dev, ORB)
                        for low in range(2)
                    ],
                    axis=1,
                )
                matrix = jnp.concatenate(
                    [
                        weights[place, near, row]
                        for row in range(2 * piece, 2 * piece + 4)
                        for near in range(NBR)
                    ],
                    axis=0,
                )
                total = total + dot(block, matrix)
            result.append(total.astype(jnp.bfloat16))
        return result

    def to_time(atom, coupled):
        time_re = dot(cos_ref[...], coupled[0]) + dot(sin_ref[...], coupled[1])
        time_im = dot(cos_ref[...], coupled[1]) - dot(sin_ref[...], coupled[0])
        time_buf[mom, atom, 0] = time_re.astype(jnp.bfloat16)
        time_buf[mom, atom, 1] = time_im.astype(jnp.bfloat16)

    def mirror_part():
        for other in range(1, mom_count):
            forward_copy(other, True).wait_send()
            forward_copy(other, False).wait_recv()
        for atom in range(shared):
            mask_coupling(mirror_buf, atom, mirror * atom_dev + atom)
        arrive_all(0)
        for atom in range(shared):
            far = couple(atom, mirror_buf, atom, half_count, half_count)
            for part in range(2):
                part_buf[atom, part] = far[part]
        part_copy(True).start()
        for phase in range(early, len(phases)):
            send_phase(phase, layers // 2, layers)
        rows = pl.ds(pl.multiple_of(my_half * half_rows, half_rows), half_rows)
        for atom in range(shared):
            near = couple(atom, coupling_buf, atom, 0, half_count)
            for part in range(2):
                coupled_buf[atom, part, rows, :] = near[part]

    def transform(phase):
        start, size = phases[phase]
        if phase == 0:
            part_copy(False).wait_recv()
            for atom in range(size):
                to_time(atom, [coupled_buf[atom, 0], coupled_buf[atom, 1]])
        else:
            arrive_all(phase)
            for atom in range(start, start + size):
                to_time(atom, couple(atom, coupling_buf, atom, 0, shard_count))
        for step in range(1, mom_count):
            mom_copy(phase, step, True).start()

    def send_phase(phase, first, stop):
        def more(step, carry):
            start_sends(phase, layer_at(step))
            return carry

        lax.fori_loop(first, stop, more, 0)

    lax.fori_loop(0, layers, layer_step, 0)
    for copy in small[4:]:
        copy.wait()
    coupling_copy().wait()
    for atom in range(atom_dev):
        mask_coupling(coupling_buf, atom, me * atom_dev + atom)
    spread_phonon()

    for phase in range(early, len(phases)):
        send_phase(phase, 0, layers // 2)
    mirror_part()
    transform(1)
    transform(0)
    finish(1)
    finish(0)
    for phase in range(2, len(phases)):
        transform(phase)
        finish(phase)

    def drain(dest, carry):
        for phase in range(max(len(phases) - early, 0), len(phases)):

            @pl.when(route(phase, dest)[0] != me)
            def _():
                send_copy(phase, dest).wait_send()

        return carry

    lax.fori_loop(0, shard_count, drain, 0)
    mirror_copy().wait_send()
    part_copy(True).wait_send()
    for phase in range(len(phases)):
        for step in range(1, mom_count):
            mom_copy(phase, step, True).wait_send()


def fused(shard_count, mom_count, green_ret, broadening, occupation, neighbours, orbitals,
          coupling, phonon, mode_table):
    greens = green_ret[0]
    energy_dev = greens.shape[0]
    atom_dev = coupling.shape[0]
    energies = phonon.shape[-1]
    counter = np.arange(energies, dtype=np.int32)
    angles = (counter[:, None] * counter[None, :] % energies).astype(np.float32)
    angles = angles * np.float32(2.0 * math.pi / energies)
    cos_table = jnp.asarray(np.cos(angles), jnp.bfloat16)
    sin_table = jnp.asarray(np.sin(angles), jnp.bfloat16)
    blocks = coupling.reshape(atom_dev, NBR, NORB, NORB, PAIR)
    shared = mom_count
    phases = phase_plan(atom_dev, shared)
    count = len(phases)
    vmem = pl.BlockSpec(memory_space=pltpu.VMEM)
    hbm = pl.BlockSpec(memory_space=pl.ANY)
    smem = pltpu.SMEM
    dma = pltpu.SemaphoreType.DMA
    result = pl.pallas_call(
        functools.partial(fused_kernel, phases, shard_count, mom_count),
        out_shape=jax.ShapeDtypeStruct((energies, atom_dev * 2 * PAIR), jnp.bfloat16),
        in_specs=[hbm] * 10,
        out_specs=vmem,
        scratch_shapes=[
            pltpu.VMEM(broadening.shape, broadening.dtype),
            smem(occupation.shape, occupation.dtype),
            smem(neighbours.shape[::-1], neighbours.dtype),
            smem(orbitals.shape, orbitals.dtype),
            pltpu.VMEM(phonon.shape, phonon.dtype),
            smem(mode_table.shape, mode_table.dtype),
            pltpu.VMEM(cos_table.shape, cos_table.dtype),
            pltpu.VMEM(sin_table.shape, sin_table.dtype),
            dma((8,)),
            pltpu.VMEM((LAYERS, energy_dev, 2, ORB, ORB), jnp.bfloat16),
            pltpu.VMEM((energy_dev, ORB, 2 * ORB), jnp.bfloat16),
            pltpu.VMEM((ATOMS, NORB, energy_dev, ORB), jnp.bfloat16),
            pltpu.VMEM((atom_dev, shard_count, NORB, energy_dev, ORB), jnp.bfloat16),
            pltpu.VMEM((atom_dev, NBR, NORB, NORB, PAIR), jnp.bfloat16),
            pltpu.VMEM((mom_count, 2, energies, ORB), jnp.float32),
            pltpu.VMEM((2 * ORB, 2 * ORB), jnp.bfloat16),
            pltpu.VMEM((energy_dev * NORB, energy_dev * NORB), jnp.bfloat16),
            pltpu.VMEM((shared, NBR, NORB, NORB, PAIR), jnp.bfloat16),
            pltpu.VMEM((shared, 2, energies, PAIR), jnp.bfloat16),
            pltpu.VMEM((shared, 2, energies // 2, PAIR), jnp.bfloat16),
            pltpu.VMEM((mom_count, atom_dev, 2, energies, PAIR), jnp.bfloat16),
            dma((LAYERS,)),
            dma,
            dma((2 * count,)),
            dma((count, shard_count)),
            dma((count, shard_count)),
            dma((count, max(mom_count - 1, 1))),
            dma((count, max(mom_count - 1, 1))),
            dma((2,)),
            dma((max(mom_count - 1, 1),)),
            dma((max(mom_count - 1, 1),)),
            dma((2,)),
        ],
        compiler_params=pltpu.CompilerParams(
            collective_id=0, has_side_effects=True, vmem_limit_bytes=56 * 1024 * 1024
        ),
    )(
        greens, broadening, occupation, neighbours.T, orbitals, blocks, phonon, mode_table,
        cos_table, sin_table,
    )
    return result.reshape(1, energies, atom_dev, 2, PAIR)


def solution(mesh):
    in_specs = (
        P("mom", "shard", None, None, None, None),
        P(),
        P("mom", "shard"),
        P(),
        P(),
        P("shard", None, None, None),
        P(),
        P(),
    )
    out_specs = P("mom", None, "shard", None, None)
    shard_count, mom_count = mesh.shape["shard"], mesh.shape["mom"]

    def body(*args):
        energy_dev, atom_dev = args[0].shape[1], args[5].shape[0]
        if energy_dev % 16 == 0 and ATL % atom_dev == 0 and atom_dev >= mom_count + 2:
            return fused(shard_count, mom_count, *args)
        return local(*args)

    return jax.shard_map(body, mesh=mesh, in_specs=in_specs, out_specs=out_specs, check_vma=False)
```

```python
import functools
import math

import jax
import jax.numpy as jnp
import numpy as np
from jax import lax
from jax.experimental import pallas as pl
from jax.experimental.pallas import tpu as pltpu
from jax.sharding import PartitionSpec as P

NORB = 16
ATL = 8
NBR = 4
ENERGIES = 256
LAYERS = 8
ORB = 128
PAIR = 256
ATOMS = 64


def dft_tables(length):
    counter = jnp.arange(length, dtype=jnp.int32)
    phases = counter[:, None] * counter[None, :] % length
    angles = phases.astype(jnp.float32) * (2.0 * math.pi / length)
    return (jnp.cos(angles).astype(jnp.bfloat16), jnp.sin(angles).astype(jnp.bfloat16))


def local(green_ret, broadening, occupation, neighbours, orbitals, coupling, phonon, mode_table):
    highest = lax.Precision.HIGHEST
    greens = green_ret[0]
    energy_dev = greens.shape[0]
    mixing = jnp.stack(
        [
            jnp.concatenate([broadening[0], broadening[1]], axis=1),
            jnp.concatenate([-broadening[1], broadening[0]], axis=1),
        ],
        axis=0,
    )
    left = jnp.einsum("elpik,pkq->eliq", greens, mixing, preferred_element_type=jnp.float32).astype(
        jnp.bfloat16
    )
    slot_atoms = neighbours % ATL
    selector = slot_atoms[:, :, None] == jnp.arange(ATL, dtype=jnp.int32)[None, None, :]
    layer_orbitals = jnp.repeat(orbitals.reshape(LAYERS, ATL), ATL, axis=0)
    partner_count = jnp.sum(jnp.where(selector, layer_orbitals[:, None, :], 0), axis=2)
    green_rows = greens.reshape(energy_dev, LAYERS, 2, ATL, NORB, ORB)
    select_bf = selector.reshape(LAYERS, ATL, NBR, ATL).astype(jnp.bfloat16)
    partner_rows = jnp.einsum(
        "ljnm,elpmic->eljnpic", select_bf, green_rows, preferred_element_type=jnp.float32
    ).astype(jnp.bfloat16)
    partner_re = partner_rows[:, :, :, :, 0]
    partner_im = partner_rows[:, :, :, :, 1]
    left_rows_re = left[..., :ORB].reshape(energy_dev, LAYERS, ATL, NORB, ORB)
    left_rows_im = left[..., ORB:].reshape(energy_dev, LAYERS, ATL, NORB, ORB)
    pair_re = jnp.einsum(
        "eljic,eljnkc->eljnik", left_rows_re, partner_re, preferred_element_type=jnp.float32
    ) + jnp.einsum(
        "eljic,eljnkc->eljnik", left_rows_im, partner_im, preferred_element_type=jnp.float32
    )
    pair_im = jnp.einsum(
        "eljic,eljnkc->eljnik", left_rows_im, partner_re, preferred_element_type=jnp.float32
    ) - jnp.einsum(
        "eljic,eljnkc->eljnik", left_rows_re, partner_im, preferred_element_type=jnp.float32
    )
    chosen = jnp.stack([pair_re, pair_im], axis=4)
    chosen = chosen.reshape(energy_dev, ATOMS, NBR, 2, NORB, NORB)
    counter = jnp.arange(NORB, dtype=jnp.int32)
    row_mask = counter[None, :] < orbitals[:, None]
    column_mask = counter[None, None, :] < partner_count[:, :, None]
    pair_mask = (row_mask[:, None, :, None] & column_mask[:, :, None, :]).astype(jnp.float32)
    scaled = (
        chosen * occupation[0][:, None, None, None, None, None] * pair_mask[None, :, :, None, :, :]
    )
    pair_blocks = scaled.reshape(energy_dev, ATOMS, NBR, 2, PAIR).astype(jnp.bfloat16)
    arrived = lax.all_to_all(pair_blocks, "shard", split_axis=1, concat_axis=0, tiled=True)
    atom_dev = arrived.shape[1]
    mixed_terms = jnp.einsum(
        "eanpx,anxy->eapy", arrived, coupling, preferred_element_type=jnp.float32
    )
    first_atom = lax.axis_index("shard") * atom_dev
    own_orbitals = lax.dynamic_slice_in_dim(orbitals, first_atom, atom_dev)
    pair_index = jnp.arange(PAIR, dtype=jnp.int32)
    own_mask = (
        (pair_index[None, :] // NORB < own_orbitals[:, None])
        & (pair_index[None, :] % NORB < own_orbitals[:, None])
    ).astype(jnp.float32)
    coupled = (mixed_terms * own_mask[None, :, None, :]).astype(jnp.bfloat16)
    cos_table, sin_table = dft_tables(ENERGIES)
    flat_coupled = coupled.reshape(ENERGIES, -1)
    part_cos = jnp.dot(cos_table, flat_coupled, preferred_element_type=jnp.float32).reshape(
        ENERGIES, atom_dev, 2, PAIR
    )
    part_sin = jnp.dot(sin_table, flat_coupled, preferred_element_type=jnp.float32).reshape(
        ENERGIES, atom_dev, 2, PAIR
    )
    time_data = jnp.stack(
        [part_cos[:, :, 0] + part_sin[:, :, 1], part_cos[:, :, 1] - part_sin[:, :, 0]], axis=2
    ).astype(jnp.bfloat16)
    own_momentum = lax.axis_index("mom")
    mode_count = phonon.shape[0]
    mode_ids = jnp.arange(mode_count, dtype=jnp.int32)
    own_modes = lax.dynamic_slice_in_dim(mode_table, own_momentum, 1, 0)[0]
    phonon_flat = phonon.reshape(mode_count, -1)
    received = lax.all_gather(time_data[None], "mom", axis=0, tiled=True)
    row_count = received.shape[0]
    one_hot = (own_modes[:, None] == mode_ids[None, :]).astype(jnp.float32)
    kernel = jnp.dot(one_hot, phonon_flat, precision=highest).reshape(row_count, 2, ENERGIES)
    values = received.astype(jnp.float32)
    kernel_re = kernel[:, 0][:, :, None, None]
    kernel_im = kernel[:, 1][:, :, None, None]
    add_re = jnp.sum(kernel_re * values[:, :, :, 0] - kernel_im * values[:, :, :, 1], axis=0)
    add_im = jnp.sum(kernel_re * values[:, :, :, 1] + kernel_im * values[:, :, :, 0], axis=0)
    summed = jnp.stack([add_re, add_im], axis=2)
    convolved = summed.astype(jnp.bfloat16)
    flat_conv = convolved.reshape(ENERGIES, -1)
    back_cos = jnp.dot(cos_table, flat_conv, preferred_element_type=jnp.float32).reshape(
        ENERGIES, atom_dev, 2, PAIR
    )
    back_sin = jnp.dot(sin_table, flat_conv, preferred_element_type=jnp.float32).reshape(
        ENERGIES, atom_dev, 2, PAIR
    )
    result_re = (back_cos[:, :, 0] - back_sin[:, :, 1]) * (1.0 / ENERGIES)
    result_im = (back_cos[:, :, 1] + back_sin[:, :, 0]) * (1.0 / ENERGIES)
    return jnp.stack([result_re, result_im], axis=2)[None].astype(jnp.bfloat16)


MESH = pl.DeviceIdType.MESH


def phase_plan(atom_dev):
    if atom_dev < 4:
        return [(start, 1) for start in range(atom_dev)]
    first = atom_dev // 2
    return [(0, first)] + [(start, 1) for start in range(first, atom_dev)]


def fused_kernel(
    phases,
    shard_count,
    mom_count,
    green_hbm,
    broadening_hbm,
    occupation_hbm,
    neighbours_hbm,
    orbitals_hbm,
    coupling_hbm,
    phonon_hbm,
    modes_hbm,
    cos_hbm,
    sin_hbm,
    out_ref,
    broadening_ref,
    occupation_ref,
    neighbours_ref,
    orbitals_ref,
    phonon_ref,
    modes_ref,
    cos_ref,
    sin_ref,
    small_sem,
    green_buf,
    full_buf,
    send_buf,
    recv_buf,
    coupling_buf,
    kernel_buf,
    mixing_ref,
    turn_ref,
    time_buf,
    green_sem,
    coupling_sem,
    own_sem,
    send_sem,
    recv_sem,
    mom_send_sem,
    mom_recv_sem,
):
    me = lax.axis_index("shard")
    mom = lax.axis_index("mom")
    layers, energy_dev = green_buf.shape[0], green_buf.shape[1]
    atom_dev = recv_buf.shape[0]
    dev_layer = ATL // atom_dev
    half = layers // 2
    pieces = NORB // 2
    last = len(phases) - 1
    early = min(2, len(phases))

    def layer_at(step):
        home = lax.div(me, dev_layer)
        side = lax.rem(lax.div(home, half) + 1 + step, 2)
        return side * half + lax.rem(home + lax.div(step, 2), half)

    def green_copy(layer):
        return pltpu.make_async_copy(
            green_hbm.at[:, layer], green_buf.at[layer], green_sem.at[layer]
        )

    def coupling_copy(slot):
        return pltpu.make_async_copy(
            coupling_hbm.at[:, slot], coupling_buf.at[:, :, slot], coupling_sem.at[slot]
        )

    def own_copy(phase):
        start, size = phases[phase]
        return pltpu.make_async_copy(
            send_buf.at[pl.ds(me * atom_dev + start, size)],
            recv_buf.at[pl.ds(start, size), me],
            own_sem.at[phase],
        )

    def send_copy(phase, dest):
        start, size = phases[phase]
        return pltpu.make_async_remote_copy(
            src_ref=send_buf.at[pl.ds(dest * atom_dev + start, size)],
            dst_ref=recv_buf.at[pl.ds(start, size), me],
            send_sem=send_sem.at[phase, dest],
            recv_sem=recv_sem.at[phase, me],
            device_id={"shard": dest},
            device_id_type=MESH,
        )

    def arrive_copy(phase, source):
        start, size = phases[phase]
        return pltpu.make_async_remote_copy(
            src_ref=send_buf.at[pl.ds(source * atom_dev + start, size)],
            dst_ref=recv_buf.at[pl.ds(start, size), source],
            send_sem=send_sem.at[phase, source],
            recv_sem=recv_sem.at[phase, source],
            device_id={"shard": source},
            device_id_type=MESH,
        )

    def mom_copy(phase, step, sending):
        start, size = phases[phase]
        dest = lax.rem(mom + step, mom_count)
        source = lax.rem(mom + mom_count - step, mom_count)
        origin = mom if sending else source
        return pltpu.make_async_remote_copy(
            src_ref=time_buf.at[mom, pl.ds(start, size)],
            dst_ref=time_buf.at[origin, pl.ds(start, size)],
            send_sem=mom_send_sem.at[phase, step - 1],
            recv_sem=mom_recv_sem.at[phase, step - 1],
            device_id={"mom": dest},
            device_id_type=MESH,
        )

    small = [
        (broadening_hbm, broadening_ref),
        (occupation_hbm, occupation_ref),
        (neighbours_hbm, neighbours_ref),
        (orbitals_hbm, orbitals_ref),
        (phonon_hbm, phonon_ref),
        (modes_hbm, modes_ref),
        (cos_hbm, cos_ref),
        (sin_hbm, sin_ref),
    ]
    small = [
        pltpu.make_async_copy(source, held, small_sem.at[index])
        for index, (source, held) in enumerate(small)
    ]
    for copy in small[:4]:
        copy.start()
    for step in range(layers):
        green_copy(layer_at(step)).start()
    for copy in small[4:]:
        copy.start()
    for slot in range(NBR):
        coupling_copy(slot).start()

    barrier = pltpu.get_barrier_semaphore()
    for step in range(1, shard_count):
        pl.semaphore_signal(
            barrier,
            inc=1,
            device_id={"shard": lax.rem(me + step, shard_count)},
            device_id_type=MESH,
        )
    for step in range(1, mom_count):
        pl.semaphore_signal(
            barrier,
            inc=1,
            device_id={"mom": lax.rem(mom + step, mom_count)},
            device_id_type=MESH,
        )
    for copy in small[:4]:
        copy.wait()
    mixing_ref[:ORB, :ORB] = broadening_ref[0]
    mixing_ref[:ORB, ORB:] = broadening_ref[1]
    mixing_ref[ORB:, :ORB] = -broadening_ref[1]
    mixing_ref[ORB:, ORB:] = broadening_ref[0]
    turn_shape = turn_ref.shape
    wanted = lax.broadcasted_iota(jnp.int32, turn_shape, 0)
    held = lax.broadcasted_iota(jnp.int32, turn_shape, 1)
    wanted = lax.rem(wanted, energy_dev) * NORB + lax.div(wanted, energy_dev)
    turn_ref[...] = jnp.where(wanted == held, 1.0, 0.0).astype(jnp.bfloat16)
    group = 8
    unroll = 4

    def layer_pairs(layer):
        green_copy(layer).wait()

        def energy_step(index, inner):
            first = index * group
            joined = [
                jnp.concatenate(
                    [green_buf[layer, first + j, 0], green_buf[layer, first + j, 1]], axis=1
                )
                for j in range(group)
            ]
            left = jnp.dot(
                jnp.concatenate(joined, axis=0),
                mixing_ref[...],
                preferred_element_type=jnp.float32,
            ).astype(jnp.bfloat16)
            for j in range(group):
                own_left = left[j * ORB : (j + 1) * ORB]
                products = lax.dot_general(
                    jnp.concatenate([own_left[:, :ORB], own_left[:, ORB:]], axis=0),
                    jnp.concatenate([joined[j][:, :ORB], joined[j][:, ORB:]], axis=0),
                    (((1,), (1,)), ((), ())),
                    preferred_element_type=jnp.float32,
                )
                full_re = products[:ORB, :ORB] + products[ORB:, ORB:]
                full_im = products[ORB:, :ORB] - products[:ORB, ORB:]
                weight = occupation_ref[0, first + j]
                full_buf[first + j, :, :ORB] = (full_re * weight).astype(jnp.bfloat16)
                full_buf[first + j, :, ORB:] = (full_im * weight).astype(jnp.bfloat16)
            return inner

        lax.fori_loop(0, energy_dev // group, energy_step, 0)

        lane = lax.broadcasted_iota(jnp.int32, (1, ORB), 1)
        lane_slot = lax.rem(lax.div(lane, NORB), NBR)
        lane_base = lax.rem(lane, NORB) + lax.div(lane, NORB * NBR) * ORB
        row_ids = lax.broadcasted_iota(jnp.int32, (2 * ORB, ORB), 0)

        def pick_atom(slot):
            atom = layer * ATL + slot
            target = lane_base
            for near in range(NBR):
                start = (neighbours_ref[near, atom] - layer * ATL) * NORB
                target = target + jnp.where(lane_slot == near, start, 0)
            rows = pl.ds(pl.multiple_of(slot * NORB, NORB), NORB)
            block = full_buf[:, rows, :].reshape(energy_dev * NORB, 2 * ORB)
            turned = jnp.dot(
                turn_ref[...], block, preferred_element_type=jnp.float32
            ).astype(jnp.bfloat16)
            strips = []
            for part in range(2):
                columns = slice(part * ORB, (part + 1) * ORB)
                for piece in range(pieces):
                    begin = 2 * piece * energy_dev
                    pair = [
                        turned[begin + low * energy_dev : begin + (low + 1) * energy_dev, columns]
                        for low in range(2)
                    ]
                    strips.append(jnp.concatenate(pair, axis=1))
            stacked = jnp.concatenate(strips, axis=0)
            chosen = jnp.where(row_ids == target, 1.0, 0.0)
            picked = jnp.dot(
                stacked, chosen.astype(jnp.bfloat16), preferred_element_type=jnp.float32
            )
            send_buf[atom] = picked.astype(jnp.bfloat16).reshape(2 * pieces, energy_dev, ORB)

        def atom_step(index, inner):
            for j in range(unroll):
                pick_atom(index * unroll + j)
            return inner

        lax.fori_loop(0, ATL // unroll, atom_step, 0)

    def layer_step(step, carry):
        layer_pairs(layer_at(step))
        for phase in range(early):
            start_sends(phase, layer_at(step))
        return carry

    def mask_coupling():
        shape = (NORB, PAIR)
        column = lax.broadcasted_iota(jnp.int32, shape, 0)
        entry = lax.broadcasted_iota(jnp.int32, shape, 1)
        outer, inner = lax.div(entry, NORB), lax.rem(entry, NORB)
        for slot in range(NBR):
            coupling_copy(slot).wait()
        for atom in range(atom_dev):
            place = me * atom_dev + atom
            own = orbitals_ref[place]
            kept = (outer < own) & (inner < own)
            masks = [
                jnp.where(kept & (column < orbitals_ref[neighbours_ref[near, place]]), 1.0, 0.0)
                for near in range(NBR)
            ]

            def row_step(row, carry):
                used = jnp.where(row < own, 1.0, 0.0)
                for near in range(NBR):
                    block = coupling_buf[atom, row, near].astype(jnp.float32)
                    coupling_buf[atom, row, near] = (block * (masks[near] * used)).astype(
                        jnp.bfloat16
                    )
                return carry

            lax.fori_loop(0, NORB, row_step, 0)

    def spread_phonon():
        for other in range(mom_count):
            mode = modes_ref[mom, other]
            rows = phonon_ref[mode]
            for part in range(2):
                wide = jnp.broadcast_to(rows[part : part + 1], (ORB, rows.shape[1]))
                kernel_buf[other, part] = wide.T

    def start_sends(phase, layer):
        for offset in range(dev_layer):
            dest = layer * dev_layer + offset

            @pl.when(dest != me)
            def _():
                if phase >= early:
                    send_copy(phase - early, dest).wait_send()
                send_copy(phase, dest).start()

            @pl.when(dest == me)
            def _():
                own_copy(phase).start()

    def finish(phase):
        start, size = phases[phase]
        for step in range(1, mom_count):
            mom_copy(phase, step, False).wait_recv()
        for atom in range(start, start + size):
            sums = [0.0, 0.0]
            for other in range(mom_count):
                wide_re = jnp.concatenate([kernel_buf[other, 0]] * (PAIR // ORB), axis=1)
                wide_im = jnp.concatenate([kernel_buf[other, 1]] * (PAIR // ORB), axis=1)
                time_re = time_buf[other, atom, 0].astype(jnp.float32)
                time_im = time_buf[other, atom, 1].astype(jnp.float32)
                sums[0] = sums[0] + (wide_re * time_re - wide_im * time_im)
                sums[1] = sums[1] + (wide_re * time_im + wide_im * time_re)
            conv_re = sums[0].astype(jnp.bfloat16)
            conv_im = sums[1].astype(jnp.bfloat16)
            dot = functools.partial(jnp.dot, preferred_element_type=jnp.float32)
            scale = 1.0 / cos_ref.shape[0]
            res_re = (dot(cos_ref[...], conv_re) - dot(sin_ref[...], conv_im)) * scale
            res_im = (dot(cos_ref[...], conv_im) + dot(sin_ref[...], conv_re)) * scale
            base = atom * 2 * PAIR
            out_ref[:, base : base + PAIR] = res_re.astype(jnp.bfloat16)
            out_ref[:, base + PAIR : base + 2 * PAIR] = res_im.astype(jnp.bfloat16)

    def transform(phase):
        start, size = phases[phase]

        def arrive(source, carry):
            @pl.when(source != me)
            def _():
                arrive_copy(phase, source).wait_recv()

            return carry

        lax.fori_loop(0, shard_count, arrive, 0)
        own_copy(phase).wait()
        energies = shard_count * energy_dev
        for atom in range(start, start + size):
            coupled = []
            for part in range(2):
                total = 0.0
                for piece in range(0, pieces, 2):
                    block = jnp.concatenate(
                        [
                            recv_buf[atom, :, part * pieces + piece + low].reshape(energies, ORB)
                            for low in range(2)
                        ],
                        axis=1,
                    )
                    total = total + jnp.dot(
                        block,
                        coupling_buf[atom, 2 * piece : 2 * piece + 4].reshape(PAIR, PAIR),
                        preferred_element_type=jnp.float32,
                    )
                coupled.append(total.astype(jnp.bfloat16))
            dot = functools.partial(jnp.dot, preferred_element_type=jnp.float32)
            time_re = dot(cos_ref[...], coupled[0]) + dot(sin_ref[...], coupled[1])
            time_im = dot(cos_ref[...], coupled[1]) - dot(sin_ref[...], coupled[0])
            time_buf[mom, atom, 0] = time_re.astype(jnp.bfloat16)
            time_buf[mom, atom, 1] = time_im.astype(jnp.bfloat16)
        for step in range(1, mom_count):
            mom_copy(phase, step, True).start()

    layer_pairs(layer_at(0))
    pl.semaphore_wait(barrier, shard_count + mom_count - 2)
    for phase in range(early):
        start_sends(phase, layer_at(0))
    lax.fori_loop(1, layers, layer_step, 0)
    for copy in small[4:]:
        copy.wait()
    mask_coupling()
    spread_phonon()

    def send_phase(phase):
        def more(step, carry):
            start_sends(phase, layer_at(step))
            return carry

        lax.fori_loop(0, layers, more, 0)

    done = 0
    for phase in range(len(phases)):
        if phase + 2 <= last and phase + 2 >= early:
            send_phase(phase + 2)
        transform(phase)
        if phase >= 2 or phase == last:
            while done < phase:
                finish(done)
                done += 1
        elif phase == 1:
            finish(0)
            done = 1
    finish(last)

    def drain(dest, carry):
        @pl.when(dest != me)
        def _():
            for phase in range(max(len(phases) - early, 0), len(phases)):
                send_copy(phase, dest).wait_send()

        return carry

    lax.fori_loop(0, shard_count, drain, 0)
    for phase in range(len(phases)):
        for step in range(1, mom_count):
            mom_copy(phase, step, True).wait_send()


def fused(shard_count, mom_count, green_ret, broadening, occupation, neighbours, orbitals,
          coupling, phonon, mode_table):
    greens = green_ret[0]
    energy_dev = greens.shape[0]
    atom_dev = coupling.shape[0]
    energies = phonon.shape[-1]
    counter = np.arange(energies, dtype=np.int32)
    angles = (counter[:, None] * counter[None, :] % energies).astype(np.float32)
    angles = angles * np.float32(2.0 * math.pi / energies)
    cos_table = jnp.asarray(np.cos(angles), jnp.bfloat16)
    sin_table = jnp.asarray(np.sin(angles), jnp.bfloat16)
    blocks = coupling.reshape(atom_dev, NBR, NORB, NORB, PAIR)
    phases = phase_plan(atom_dev)
    count = len(phases)
    vmem = pl.BlockSpec(memory_space=pltpu.VMEM)
    hbm = pl.BlockSpec(memory_space=pl.ANY)
    smem = pltpu.SMEM
    dma = pltpu.SemaphoreType.DMA
    result = pl.pallas_call(
        functools.partial(fused_kernel, phases, shard_count, mom_count),
        out_shape=jax.ShapeDtypeStruct((energies, atom_dev * 2 * PAIR), jnp.bfloat16),
        in_specs=[hbm] * 10,
        out_specs=vmem,
        scratch_shapes=[
            pltpu.VMEM(broadening.shape, broadening.dtype),
            smem(occupation.shape, occupation.dtype),
            smem(neighbours.shape[::-1], neighbours.dtype),
            smem(orbitals.shape, orbitals.dtype),
            pltpu.VMEM(phonon.shape, phonon.dtype),
            smem(mode_table.shape, mode_table.dtype),
            pltpu.VMEM(cos_table.shape, cos_table.dtype),
            pltpu.VMEM(sin_table.shape, sin_table.dtype),
            dma((8,)),
            pltpu.VMEM((LAYERS, energy_dev, 2, ORB, ORB), jnp.bfloat16),
            pltpu.VMEM((energy_dev, ORB, 2 * ORB), jnp.bfloat16),
            pltpu.VMEM((ATOMS, NORB, energy_dev, ORB), jnp.bfloat16),
            pltpu.VMEM((atom_dev, shard_count, NORB, energy_dev, ORB), jnp.bfloat16),
            pltpu.VMEM((atom_dev, NORB, NBR, NORB, PAIR), jnp.bfloat16),
            pltpu.VMEM((mom_count, 2, energies, ORB), jnp.float32),
            pltpu.VMEM((2 * ORB, 2 * ORB), jnp.bfloat16),
            pltpu.VMEM((energy_dev * NORB, energy_dev * NORB), jnp.bfloat16),
            pltpu.VMEM((mom_count, atom_dev, 2, energies, PAIR), jnp.bfloat16),
            dma((LAYERS,)),
            dma((NBR,)),
            dma((count,)),
            dma((count, shard_count)),
            dma((count, shard_count)),
            dma((count, max(mom_count - 1, 1))),
            dma((count, max(mom_count - 1, 1))),
        ],
        compiler_params=pltpu.CompilerParams(
            collective_id=0, has_side_effects=True, vmem_limit_bytes=56 * 1024 * 1024
        ),
    )(
        greens, broadening, occupation, neighbours.T, orbitals, blocks, phonon, mode_table,
        cos_table, sin_table,
    )
    return result.reshape(1, energies, atom_dev, 2, PAIR)


def solution(mesh):
    in_specs = (
        P("mom", "shard", None, None, None, None),
        P(),
        P("mom", "shard"),
        P(),
        P(),
        P("shard", None, None, None),
        P(),
        P(),
    )
    out_specs = P("mom", None, "shard", None, None)
    shard_count, mom_count = mesh.shape["shard"], mesh.shape["mom"]

    def body(*args):
        energy_dev, atom_dev = args[0].shape[1], args[5].shape[0]
        if energy_dev % 16 == 0 and ATL % atom_dev == 0:
            return fused(shard_count, mom_count, *args)
        return local(*args)

    return jax.shard_map(body, mesh=mesh, in_specs=in_specs, out_specs=out_specs, check_vma=False)
```
